256 devices in a mesh: dp: 8 (over z), seq: 32 (over x, y, core).
Axes of the slice: x: 4, y: 4, z: 8, core: 2. Of those that a mesh axis runs over, the one named last changes fastest.
Arguments:
- x_rows: bfloat16 [8, 4096, 1024], P('dp', 'seq'), may hold values from -6 to 6
- lengths: int32 [8, 8], P('dp'), may hold values from 1 to 2048, 4096 in all within a row
- targets: int32 [8, 8], P('dp'), may hold values from 1 to 64
- w_in: bfloat16 [1024, 2048], replicated, may hold values from -0.1875 to 0.1875
- w_out: bfloat16 [512, 1024], replicated, may hold values from -0.25 to 0.25
- w_score: bfloat16 [1024, 256], replicated, may hold values from -0.1875 to 0.1875
- head_score: float32 [256], replicated, may hold values from -0.375 to 0.375
- grad_out: bfloat16 [8, 4096, 1024], P('dp', 'seq'), may hold values from -6 to 6
- grad_score: float32 [8, 4096], P('dp', 'seq'), may hold values from -6 to 6
Outputs:
- d_x: bfloat16 [8, 4096, 1024], P('dp', 'seq')
- d_w_in: float32 [1024, 2048], P('seq', 'dp')
- d_w_out: float32 [512, 1024], P('seq', 'dp')
- d_w_score: float32 [1024, 256], P('seq', 'dp')
- d_head: float32 [256], replicated
The draws below stay inside these ranges and needn't reach their ends.
Inputs may be any that keep to these rules, and one draw needn't show every extreme that they name: Each row lists the lengths of 8 histories packed end to end in the 4096 positions of a group; they sum to 4096 and the largest is 2048.
All inputs are finite; a program needn't handle non-finite values.
Results may differ from the reference program's by a relative error of at most 0.0084.
Values may be sent and summed in bfloat16 or wider, within the bound.
No kernel may reach another device: no remote copies, remote signals or barrier semaphores. Data moves between devices by JAX's collectives and lax.ppermute only.
A program may use at most 64 MiB of HBM per device.

```python
import math
import jax
import jax.numpy as jnp
import numpy as np
from jax import lax

D = 1024
HEADS = 4
DH = 128
DM = 256
HIST = 8
TGT = 64
TOKENS = 4096
MOST = 2048
GROUPS = 8


def with_ends(values, rng, low, largest):
    longest = values.shape.index(max(values.shape))
    spots = []
    for shift in (0, 1):
        where = [jax.random.randint(jax.random.fold_in(rng, axis), (), 0, length) for axis, length in enumerate(values.shape)]
        where[longest] = (where[longest] + shift) % values.shape[longest]
        spots.append(tuple(where))
    return values.at[spots[0]].set(low).at[spots[1]].set(largest)


def levels(own_key, extent, shards, low, largest):
    def one(axis_at, blocks):
        steps = jax.random.uniform(jax.random.fold_in(jax.random.fold_in(own_key, 6), axis_at), (blocks,), jnp.float32, low / len(shards), largest / len(shards))
        return jnp.repeat(jnp.exp(steps), extent[axis_at] // blocks).reshape((-1,) + (1,) * (len(extent) - axis_at - 1))

    level = one(*shards[0])
    for cut in shards[1:]:
        level = level * one(*cut)
    return level


def profile(count, total, bound, skew):
    weights = [(1 << 20) // math.isqrt(rank ** skew) + 1 for rank in range(2, count + 1)]
    spare, given = total - bound - (count - 1), [1] * (count - 1)
    while spare > 0:
        candidates = [i for i in range(count - 1) if given[i] < bound]
        pool, budget = sum([weights[i] for i in candidates]), spare
        for i in candidates:
            addition = min(bound - given[i], max(1, budget * weights[i] // pool), spare)
            given[i] = given[i] + addition
            spare = spare - addition
    return np.array([bound] + given)


def ragged(own_key, count, total, limit, skew):
    if count == 2:
        one = jax.random.randint(own_key, (), max(1, total - limit), min(limit, total - 1) + 1)
        return jnp.stack([one, total - one])
    tallies = jnp.asarray(profile(count, total, limit, skew), jnp.int32)
    couples = (count - 1) // 2
    giver, sink = tallies[1:1 + 2 * couples:2], tallies[2:2 + 2 * couples:2]
    slack = jnp.minimum(giver - 1, limit - sink)
    moved = jax.random.randint(jax.random.fold_in(own_key, 1), (couples,), 0, 1 << 20) % (slack + 1)
    tallies = tallies.at[1:1 + 2 * couples:2].set(giver - moved).at[2:2 + 2 * couples:2].set(sink + moved)
    return tallies[jax.random.permutation(jax.random.fold_in(own_key, 2), count)]


def normal_values(rng, shape, scale, most, shards=(), kind=jnp.bfloat16):
    values = jax.random.normal(rng, shape, jnp.float32) * scale
    if len(shards) > 0:
        values = levels(rng, shape, shards, -0.22, 0.18) * values
    return jnp.clip(values, min=-most, max=most).astype(kind)


def setup_inputs(seed: int = 0) -> dict:
    arg_keys = jax.random.split(jax.random.key(seed), 10)
    return {
        "x_rows": normal_values(arg_keys[0], (GROUPS, TOKENS, D), 1.0, 6.0, ((0, 8), (1, 32))),
        "lengths": jax.vmap(lambda own: ragged(own, HIST, TOKENS, MOST, 2))(jax.random.split(arg_keys[1], GROUPS)).reshape((GROUPS, HIST)).astype(jnp.int32),
        "targets": with_ends(jax.random.randint(arg_keys[2], (GROUPS, HIST), 1, TGT + 1), jax.random.fold_in(arg_keys[2], 1), 1, TGT).astype(jnp.int32),
        "w_in": normal_values(arg_keys[3], (D, 4 * HEADS * DH), D ** -0.5, 0.1875),
        "w_out": normal_values(arg_keys[4], (HEADS * DH, D), (HEADS * DH) ** -0.5, 0.25),
        "w_score": normal_values(arg_keys[5], (D, DM), D ** -0.5, 0.1875),
        "head_score": normal_values(arg_keys[6], (DM,), DM ** -0.5, 0.375, (), jnp.float32),
        "grad_out": normal_values(arg_keys[7], (GROUPS, TOKENS, D), 1.0, 6.0, ((0, 8), (1, 32))),
        "grad_score": normal_values(arg_keys[8], (GROUPS, TOKENS), 1.0, 6.0, ((0, 8), (1, 32)), jnp.float32),
    }


NORM_EPS = 1e-05

def silu_slope(value):
    sigma = jax.nn.sigmoid(value)
    return sigma * (1.0 + value * (1.0 - sigma))

def norm_rows(value):
    centre = value - lax.optimization_barrier(jnp.mean(value, axis=-1, keepdims=True))
    inverse = lax.rsqrt(lax.optimization_barrier(jnp.mean(centre * centre, axis=-1, keepdims=True)) + NORM_EPS)
    return (centre * inverse, inverse)

def norm_back(grad, normed, inverse):
    return inverse * (grad - lax.optimization_barrier(jnp.mean(grad, axis=-1, keepdims=True)) - normed * lax.optimization_barrier(jnp.mean(grad * normed, axis=-1, keepdims=True)))

def row_marks(positions, lengths, targets):
    ends = jnp.cumsum(lengths).astype(jnp.int32)
    starts = ends - lengths
    counts = jnp.minimum(targets, lengths - 1)
    inside = (positions[:, None] >= starts[None, :]) & (positions[:, None] < ends[None, :])
    segment = lax.optimization_barrier(jnp.sum((positions[:, None] >= ends[None, :]).astype(jnp.int32), axis=1))
    first_target = lax.optimization_barrier(jnp.sum(jnp.where(inside, (ends - counts)[None, :], 0), axis=1))
    return (segment, positions >= first_target)

def visible(query_pos, query_seg, key_pos, key_seg, key_tgt):
    same_hist = query_seg[:, None] == key_seg[None, :]
    causal = key_pos[None, :] <= query_pos[:, None]
    open_key = jnp.logical_not(key_tgt)[None, :] | (key_pos[None, :] == query_pos[:, None])
    return (same_hist & causal & open_key)[None, :, :]

def weights_of(query_b, key_b, mask, divisor):
    raw_scores = jnp.einsum('rhd,chd->hrc', query_b.astype(jnp.float32), key_b.astype(jnp.float32)) * DH ** (-0.5)
    attn_b = jnp.where(mask, jax.nn.silu(raw_scores) / divisor, 0.0).astype(jnp.bfloat16)
    return (raw_scores, attn_b)

def score_grads(raw_scores, mask, grad_b, value_b, divisor):
    grad_attn = jnp.einsum('rhd,chd->hrc', grad_b.astype(jnp.float32), value_b.astype(jnp.float32))
    factor = jnp.where(mask, silu_slope(raw_scores) * DH ** (-0.5) / divisor, 0.0)
    return (grad_attn * factor).astype(jnp.bfloat16)

def group_grads(x_rows, lengths, targets, grad_out, grad_score, w_in, w_out, w_score, head_score):
    width = HEADS * DH
    positions = jnp.arange(TOKENS, dtype=jnp.int32)
    segment, target = row_marks(positions, lengths, targets)
    divisor = float(TOKENS // 2)
    x_float = x_rows.astype(jnp.float32)
    normed, inverse = norm_rows(x_float)
    normed_b = normed.astype(jnp.bfloat16)
    pre_act = jnp.dot(normed_b, w_in, preferred_element_type=jnp.float32)
    hidden_b = jax.nn.silu(pre_act).astype(jnp.bfloat16)
    gate_b = hidden_b[:, 0:width]
    value_b = hidden_b[:, width:2 * width].reshape(TOKENS, HEADS, DH)
    query_b = hidden_b[:, 2 * width:3 * width].reshape(TOKENS, HEADS, DH)
    key_b = hidden_b[:, 3 * width:4 * width].reshape(TOKENS, HEADS, DH)
    block_rows = math.gcd(512, TOKENS)
    block_count = TOKENS // block_rows

    def query_slice(array, number):
        return lax.dynamic_slice_in_dim(array, number * block_rows, block_rows, 0)

    def forward_block(number):
        block_pos = query_slice(positions, number)
        mask = visible(block_pos, query_slice(segment, number), positions, segment, target)
        raw_scores, attn_b = weights_of(query_slice(query_b, number), key_b, mask, divisor)
        return jnp.einsum('hrc,chd->rhd', attn_b.astype(jnp.float32), value_b.astype(jnp.float32))
    attended = lax.map(forward_block, jnp.arange(block_count, dtype=jnp.int32)).reshape(TOKENS, width)
    onorm, att_inverse = norm_rows(attended)
    gate_f = gate_b.astype(jnp.float32)
    gated_b = (onorm * gate_f).astype(jnp.bfloat16)
    output = x_float + jnp.dot(gated_b, w_out, preferred_element_type=jnp.float32)
    out_b = output.astype(jnp.bfloat16)
    mid_act = jnp.dot(out_b, w_score, preferred_element_type=jnp.float32)
    weight_c = grad_score * target.astype(jnp.float32)
    head_part = lax.optimization_barrier(jnp.sum(weight_c[:, None] * jax.nn.silu(mid_act), axis=0))
    d_mid_b = (weight_c[:, None] * head_score[None, :] * silu_slope(mid_act)).astype(jnp.bfloat16)
    score_part = jnp.dot(out_b.T, d_mid_b, preferred_element_type=jnp.float32)
    d_total = grad_out.astype(jnp.float32) + jnp.dot(d_mid_b, w_score.T, preferred_element_type=jnp.float32)
    d_total_b = d_total.astype(jnp.bfloat16)
    out_part = jnp.dot(gated_b.T, d_total_b, preferred_element_type=jnp.float32)
    d_gated = jnp.dot(d_total_b, w_out.T, preferred_element_type=jnp.float32)
    d_gate = d_gated * onorm
    d_att_b = norm_back(d_gated * gate_f, onorm, att_inverse).astype(jnp.bfloat16).reshape(TOKENS, HEADS, DH)

    def query_grad_block(number):
        block_pos = query_slice(positions, number)
        mask = visible(block_pos, query_slice(segment, number), positions, segment, target)
        raw_scores, attn_b = weights_of(query_slice(query_b, number), key_b, mask, divisor)
        d_raw_b = score_grads(raw_scores, mask, query_slice(d_att_b, number), value_b, divisor)
        return jnp.einsum('hrc,chd->rhd', d_raw_b.astype(jnp.float32), key_b.astype(jnp.float32))

    def key_grad_block(number):
        key_pos = query_slice(positions, number)
        mask = visible(positions, segment, key_pos, query_slice(segment, number), query_slice(target, number))
        key_blk = query_slice(key_b, number)
        value_blk = query_slice(value_b, number)
        raw_scores, attn_b = weights_of(query_b, key_blk, mask, divisor)
        d_raw_b = score_grads(raw_scores, mask, d_att_b, value_blk, divisor)
        d_key = jnp.einsum('hrc,rhd->chd', d_raw_b.astype(jnp.float32), query_b.astype(jnp.float32))
        d_value = jnp.einsum('hrc,rhd->chd', attn_b.astype(jnp.float32), d_att_b.astype(jnp.float32))
        return (d_key, d_value)
    d_query = lax.map(query_grad_block, jnp.arange(block_count, dtype=jnp.int32)).reshape(TOKENS, width)
    d_key, d_value = lax.map(key_grad_block, jnp.arange(block_count, dtype=jnp.int32))
    d_hidden = jnp.concatenate([d_gate, d_value.reshape(TOKENS, width), d_query, d_key.reshape(TOKENS, width)], axis=1)
    d_pre_b = (d_hidden * silu_slope(pre_act)).astype(jnp.bfloat16)
    in_part = jnp.dot(normed_b.T, d_pre_b, preferred_element_type=jnp.float32)
    d_normed = jnp.dot(d_pre_b, w_in.T, preferred_element_type=jnp.float32)
    d_x = (d_total + norm_back(d_normed, normed, inverse)).astype(jnp.bfloat16)
    return (d_x, in_part, out_part, score_part, head_part)

def reference(x_rows, lengths, targets, w_in, w_out, w_score, head_score, grad_out, grad_score):

    def one_group(items):
        return group_grads(items[0], items[1], items[2], items[3], items[4], w_in, w_out, w_score, head_score)
    d_x, in_parts, out_parts, score_parts, head_parts = lax.map(one_group, (x_rows, lengths, targets, grad_out, grad_score))
    return (d_x, lax.optimization_barrier(jnp.sum(in_parts, axis=0)), lax.optimization_barrier(jnp.sum(out_parts, axis=0)), lax.optimization_barrier(jnp.sum(score_parts, axis=0)), lax.optimization_barrier(jnp.sum(head_parts, axis=0)))
```

```python
import functools

import jax
import jax.numpy as jnp
from jax import lax
from jax.experimental import pallas as pl
from jax.experimental.pallas import tpu as pltpu
from jax.sharding import Mesh
from jax.sharding import PartitionSpec as P

HEADS = 4
DH = 128
ROWS = 128
HIST = 8
TOKENS = 4096
DIVISOR = 2048.0
TILE = 256
PAIR = 2
NORM_EPS = 1e-05
SEQ = ("x", "y", "core")

f32 = jnp.float32
bf16 = jnp.bfloat16
VMEM = pl.BlockSpec(memory_space=pltpu.VMEM)
SMEM = pl.BlockSpec(memory_space=pltpu.SMEM)
HBM = pl.BlockSpec(memory_space=pltpu.HBM)
PARAMS = pltpu.CompilerParams(vmem_limit_bytes=16 * 1024 * 1024)


def cost(us):
    return pl.CostEstimate(flops=int(us * 1.15e9), bytes_accessed=0, transcendentals=0)


def shape(dims, kind):
    return jax.ShapeDtypeStruct(dims, kind)


def dot(a, b):
    return lax.dot_general(a, b, (((1,), (0,)), ((), ())), preferred_element_type=f32)


def dot_t(a, b):
    return lax.dot_general(a, b, (((1,), (1,)), ((), ())), preferred_element_type=f32)


def sigmoid(value):
    return 0.5 + 0.5 * jnp.tanh(0.5 * value)


def silu_slope(value):
    sigma = sigmoid(value)
    return sigma * (1.0 + value * (1.0 - sigma))


def norm_rows(value):
    centre = value - jnp.mean(value, axis=-1, keepdims=True)
    inverse = lax.rsqrt(jnp.mean(centre * centre, axis=-1, keepdims=True) + NORM_EPS)
    return centre * inverse, inverse


def norm_back(grad, normed, inverse):
    return inverse * (
        grad
        - jnp.mean(grad, axis=-1, keepdims=True)
        - normed * jnp.mean(grad * normed, axis=-1, keepdims=True)
    )


class Histories:
    def __init__(self, len_ref, tgt_ref):
        self.starts, self.ends, self.firsts = [], [], []
        total = jnp.int32(0)
        for h in range(HIST):
            length = len_ref[h]
            self.starts.append(total)
            total = total + length
            self.ends.append(total)
            self.firsts.append(total - jnp.minimum(tgt_ref[h], length - 1))

    def pick(self, values, pos):
        out = jnp.where(pos >= self.starts[1], values[1], values[0])
        for h in range(2, HIST):
            out = jnp.where(pos >= self.starts[h], values[h], out)
        return out

    def range_of(self, pos):
        return self.pick(self.starts, pos), jnp.minimum(self.pick(self.firsts, pos), pos + 1)


def copy_all(copies):
    for copy in copies:
        copy.start()
    return copies


def project_kernel(idx, x_hbm, w_hbm, normed_ref, o0, o1, o2, o3, x_ref, w_ref, sems):
    width = HEADS * DH
    copies = copy_all(
        [pltpu.make_async_copy(x_hbm, x_ref, sems.at[3])]
        + [
            pltpu.make_async_copy(w_hbm.at[:, pl.ds(kind * width, width)], w_ref.at[i], sems.at[i])
            for i, kind in enumerate((3, 1, 2))
        ]
    )
    copies[0].wait()
    value, _ = norm_rows(x_ref[...].astype(f32))
    normed = value.astype(bf16)
    normed_ref[...] = normed
    for i in range(3):
        copies[i + 1].wait()
        pre = dot(normed, w_ref[i])
        hidden = (pre * sigmoid(pre)).astype(bf16)
        for h in range(HEADS):
            away = lax.rem(h - idx[0] + HEADS, HEADS)
            for k, ref in enumerate((o0, o1, o2, o3)):

                @pl.when(away == k)
                def _(ref=ref, h=h):
                    ref[:, i * DH : (i + 1) * DH] = hidden[:, h * DH : (h + 1) * DH]


def project(idx, x, w_in):
    out = pl.pallas_call(
        project_kernel,
        in_specs=[SMEM, HBM, HBM],
        out_specs=[VMEM] * 5,
        out_shape=[shape((ROWS, 1024), bf16)] + [shape((ROWS, 3 * DH), bf16)] * 4,
        scratch_shapes=[
            pltpu.VMEM((ROWS, 1024), bf16),
            pltpu.VMEM((3, 1024, HEADS * DH), bf16),
            pltpu.SemaphoreType.DMA((4,)),
        ],
        compiler_params=pltpu.CompilerParams(vmem_limit_bytes=60 * 1024 * 1024),
        cost_estimate=cost(3),
        name="project",
    )(idx, x, w_in)
    return out[0], out[1:5]


def gates_kernel(normed_ref, w_hbm, gate_ref, slope_ref, w_ref, sem):
    copy = pltpu.make_async_copy(w_hbm.at[:, pl.ds(0, HEADS * DH)], w_ref, sem)
    copy.start()
    copy.wait()
    pre = dot(normed_ref[...], w_ref[...])
    sigma = sigmoid(pre)
    gate_ref[...] = (pre * sigma).astype(bf16)
    slope_ref[...] = sigma * (1.0 + pre * (1.0 - sigma))


def gates(normed, w_in):
    width = HEADS * DH
    return pl.pallas_call(
        gates_kernel,
        in_specs=[VMEM, HBM],
        out_specs=[VMEM] * 2,
        out_shape=[shape((ROWS, width), bf16), shape((ROWS, width), f32)],
        scratch_shapes=[pltpu.VMEM((1024, width), bf16), pltpu.SemaphoreType.DMA],
        compiler_params=PARAMS,
        cost_estimate=cost(2),
        name="gates",
    )(normed, w_in)


def slopes_kernel(idx, n0, n1, n2, n3, w_hbm, out_ref, w_ref, sems):
    copies = []
    for i, kind in enumerate((2, 3, 1)):
        at = pl.ds(pl.multiple_of((kind * HEADS + idx[0]) * DH, DH), DH)
        copies.append(pltpu.make_async_copy(w_hbm.at[:, at], w_ref.at[i], sems.at[i]))
    copy_all(copies)
    for i in range(3):
        copies[i].wait()
        for k, ref in enumerate((n0, n1, n2, n3)):
            out_ref[k, :, i * DH : (i + 1) * DH] = silu_slope(dot(ref[...], w_ref[i]))


def slopes(idx, normed, w_in):
    return pl.pallas_call(
        slopes_kernel,
        in_specs=[SMEM] + [VMEM] * 4 + [HBM],
        out_specs=VMEM,
        out_shape=shape((4, ROWS, 3 * DH), f32),
        scratch_shapes=[pltpu.VMEM((3, 1024, DH), bf16), pltpu.SemaphoreType.DMA((3,))],
        compiler_params=PARAMS,
        cost_estimate=cost(2.5),
        name="slopes",
    )(idx, *normed, w_in)


def block_of(idx, k):
    return lax.rem(idx[0] - k + 4, 4) * 8 + idx[1] * 2 + idx[2]


def assemble(idx, pieces, outs):
    for j in range(8):
        at_y = lax.rem(idx[1] - j % 4 + 4, 4)
        at_core = idx[2] if j < 4 else 1 - idx[2]
        for k in range(4):
            block = lax.rem(idx[0] - k + 4, 4) * 8 + at_y * 2 + at_core
            where = pl.ds(pl.multiple_of(block * ROWS, ROWS), ROWS)
            for ref, column in outs:
                ref[where, :] = pieces[j][k, :, column : column + DH]


def for_items(lows, highs, body):
    ends, total = [], jnp.int32(0)
    for low, high in zip(lows, highs, strict=True):
        total = total + (high - low + 1)
        ends.append(total)

    def step(i, carry):
        for j in range(PAIR):
            n = i * PAIR + j
            k, t = jnp.int32(0), n + lows[0]
            for q in range(1, 4):
                k = jnp.where(n >= ends[q - 1], q, k)
                t = jnp.where(n >= ends[q - 1], n - ends[q - 1] + lows[q], t)
            body(k, t, n < total)
        return carry

    lax.fori_loop(0, (total + PAIR - 1) // PAIR, step, 0)


def tile_at(t):
    return pl.ds(pl.multiple_of(jnp.minimum(t, TOKENS // TILE - 1) * TILE, TILE), TILE)


def set_marks(idx, hist, marks):
    row = lax.broadcasted_iota(jnp.int32, (ROWS, TILE), 0)
    lows, highs = [], []
    for k in range(4):
        first = block_of(idx, k) * ROWS
        start, limit = hist.range_of(first + row)
        marks[0, k], marks[1, k] = start, limit
        lows.append(hist.pick(hist.starts, first) // TILE)
        highs.append(first // TILE)
    return lows, highs


def seen_by(idx, marks, k, t):
    row = lax.broadcasted_iota(jnp.int32, (ROWS, TILE), 0)
    lane = lax.broadcasted_iota(jnp.int32, (ROWS, TILE), 1)
    key = lane + t * TILE
    return ((key >= marks[0, k]) & (key < marks[1, k])) | (key - row == block_of(idx, k) * ROWS)


def forward_kernel(idx, len_ref, tgt_ref, *refs):
    q_refs, pieces, o_refs, (k_hbm, v_hbm) = refs[0:4], refs[4:12], refs[12:16], refs[16:18]
    k_all, v_all, q_own, total, marks, sems = refs[18:24]
    hist = Histories(len_ref, tgt_ref)
    assemble(idx, pieces, [(k_all, 0), (v_all, DH)])
    copies = copy_all(
        [
            pltpu.make_async_copy(k_all, k_hbm, sems.at[0]),
            pltpu.make_async_copy(v_all, v_hbm, sems.at[1]),
        ]
    )
    for k in range(4):
        q_own[k] = q_refs[k][:, 2 * DH : 3 * DH]
    total[...] = jnp.zeros_like(total)
    lows, highs = set_marks(idx, hist, marks)

    def body(k, t, valid):
        at = tile_at(t)
        half = dot_t(q_own[k], k_all[at, :]) * (0.5 * DH**-0.5)
        weight = half * (1.0 + jnp.tanh(half))
        weight = jnp.where(seen_by(idx, marks, k, t), weight, 0.0).astype(bf16)
        total[k] += dot(weight, v_all[at, :])

    for_items(lows, highs, body)
    for k in range(4):
        o_refs[k][...] = total[k] * (1.0 / DIVISOR)
    for copy in copies:
        copy.wait()


def forward(idx, lengths, targets, queries, pieces):
    return pl.pallas_call(
        forward_kernel,
        in_specs=[SMEM] * 3 + [VMEM] * 12,
        out_specs=[VMEM] * 4 + [HBM] * 2,
        out_shape=[shape((ROWS, DH), f32)] * 4 + [shape((TOKENS, DH), bf16)] * 2,
        scratch_shapes=[pltpu.VMEM((TOKENS, DH), bf16)] * 2
        + [
            pltpu.VMEM((4, ROWS, DH), bf16),
            pltpu.VMEM((4, ROWS, DH), f32),
            pltpu.VMEM((2, 4, ROWS, TILE), jnp.int32),
            pltpu.SemaphoreType.DMA((2,)),
        ],
        compiler_params=PARAMS,
        cost_estimate=cost(5),
        name="forward",
    )(idx, lengths, targets, *queries, *pieces)


def two_of(head):
    high = head.astype(bf16).astype(f32)
    return high, (head - high).astype(bf16).astype(f32)


def with_head(rows, head, count):
    high, low = two_of(head)
    width = ACTS if rows is None else rows.shape[1]
    line = jnp.concatenate([high, low, jnp.zeros((1, width - 512), f32)], axis=1)
    line = jnp.concatenate([line, jnp.zeros((count - 1, width), f32)], axis=0)
    return (line if rows is None else jnp.concatenate([rows, line], axis=0)).astype(bf16)


def head_of(value, row):
    return value[row : row + 1, 0:256] + value[row : row + 1, 256:512]


ACTS = 512 + 1024 + 1024 + 256


def middle_kernel(idx, len_ref, tgt_ref, a0, a1, a2, a3, gate_ref, slope_ref, x_ref, w_out, w_score, head, grad, score, *refs):
    d_refs, g_full, acts, mid_ref = refs[0:4], refs[4], refs[5], refs[6]
    att, work = refs[7:9]
    for k, ref in enumerate((a0, a1, a2, a3)):
        at = pl.ds(pl.multiple_of(lax.rem(idx[0] + k, 4) * DH, DH), DH)
        att[:, at] = ref[...]
    onorm, inverse = norm_rows(att[...])
    gate = gate_ref[...].astype(f32)
    gated = (onorm * gate).astype(bf16)
    acts[0:ROWS, 0:512] = gated
    out_b = (x_ref[...].astype(f32) + dot(gated, w_out[...])).astype(bf16)
    acts[0:ROWS, 1536:2560] = out_b
    mid = dot(out_b, w_score[...])
    hist = Histories(len_ref, tgt_ref)
    own = ((idx[0] * 4 + idx[1]) * 2 + idx[2]) * ROWS
    pos = own + lax.broadcasted_iota(jnp.int32, (ROWS, 1), 0)
    weight = jnp.where(pos >= hist.pick(hist.firsts, pos), score[...], 0.0)
    sigma = sigmoid(mid)
    head_part = jnp.sum(weight * (mid * sigma), axis=0, keepdims=True)
    acts[ROWS : ROWS + 16, :] = with_head(None, head_part, 16)
    d_mid = (weight * head[...] * (sigma * (1.0 + mid * (1.0 - sigma)))).astype(bf16)
    acts[0:ROWS, 2560:2816] = d_mid
    mid_ref[...] = d_mid
    total_b = (grad[...].astype(f32) + dot_t(d_mid, w_score[...])).astype(bf16)
    acts[0:ROWS, 512:1536] = total_b
    d_gated = dot_t(total_b, w_out[...])
    att[...] = norm_back(d_gated * gate, onorm, inverse)
    work[...] = d_gated * onorm * slope_ref[...]
    g_full[...] = work[...].astype(bf16)
    for k in range(4):
        at = pl.ds(pl.multiple_of(lax.rem(idx[0] + k, 4) * DH, DH), DH)
        d_refs[k][:, 0:DH] = att[:, at].astype(bf16)
        d_refs[k][:, DH : 2 * DH] = work[:, at].astype(bf16)


def middle(idx, lengths, targets, attended, gate, slope, x, w_out, w_score, head, grad, score):
    width = HEADS * DH
    return pl.pallas_call(
        middle_kernel,
        in_specs=[SMEM] * 3 + [VMEM] * 12,
        out_specs=[VMEM] * 7,
        out_shape=[shape((ROWS, 2 * DH), bf16)] * 4
        + [
            shape((ROWS, width), bf16),
            shape((ROWS + 16, ACTS), bf16),
            shape((ROWS, 256), bf16),
        ],
        scratch_shapes=[pltpu.VMEM((ROWS, width), f32)] * 2,
        compiler_params=PARAMS,
        cost_estimate=cost(2.5),
        name="middle",
    )(idx, lengths, targets, *attended, gate, slope, x, w_out, w_score, head, grad, score)


SLOPE_SCALE = 0.5 * 2**-0.5
SLOPE_REST = DH**-0.5 / DIVISOR / 2**-0.5


def query_kernel(idx, len_ref, tgt_ref, *refs):
    q_refs, d_refs, (k_hbm, v_hbm, slope_ref), out_refs = refs[0:4], refs[4:8], refs[8:11], refs[11:15]
    k_all, v_all, q_own, d_own, total, marks, sems = refs[15:22]
    copies = copy_all(
        [
            pltpu.make_async_copy(k_hbm, k_all, sems.at[0]),
            pltpu.make_async_copy(v_hbm, v_all, sems.at[1]),
        ]
    )
    hist = Histories(len_ref, tgt_ref)
    for k in range(4):
        q_own[k] = q_refs[k][:, 2 * DH : 3 * DH]
        d_own[k] = d_refs[k][:, 0:DH]
    total[...] = jnp.zeros_like(total)
    lows, highs = set_marks(idx, hist, marks)
    for copy in copies:
        copy.wait()

    def body(k, t, valid):
        at = tile_at(t)
        keys = k_all[at, :]
        half = dot_t(q_own[k], keys) * (0.5 * DH**-0.5)
        d_attn = dot_t(d_own[k], v_all[at, :])
        tanh = jnp.tanh(half)
        factor = (SLOPE_SCALE + SLOPE_SCALE * tanh) * (1.0 + half * (1.0 - tanh))
        d_raw = jnp.where(seen_by(idx, marks, k, t), d_attn * factor, 0.0).astype(bf16)
        total[k] += dot(d_raw, keys)

    for_items(lows, highs, body)
    for k in range(4):
        out_refs[k][...] = (total[k] * SLOPE_REST * slope_ref[k, :, 0:DH]).astype(bf16)


def query_grads(idx, lengths, targets, queries, d_att, k_all, v_all, slope):
    return pl.pallas_call(
        query_kernel,
        in_specs=[SMEM] * 3 + [VMEM] * 8 + [HBM] * 2 + [VMEM],
        out_specs=[VMEM] * 4,
        out_shape=[shape((ROWS, DH), bf16)] * 4,
        scratch_shapes=[pltpu.VMEM((TOKENS, DH), bf16)] * 2
        + [pltpu.VMEM((4, ROWS, DH), bf16)] * 2
        + [
            pltpu.VMEM((4, ROWS, DH), f32),
            pltpu.VMEM((2, 4, ROWS, TILE), jnp.int32),
            pltpu.SemaphoreType.DMA((2,)),
        ],
        compiler_params=PARAMS,
        cost_estimate=cost(6),
        name="query_grads",
    )(idx, lengths, targets, *queries, *d_att, k_all, v_all, slope)


def key_kernel(idx, len_ref, tgt_ref, *refs):
    q_pieces, d_pieces, (k_hbm, v_hbm, slope_ref) = refs[0:8], refs[8:16], refs[16:19]
    dq_refs, d_refs, back_refs, all_ref = refs[19:23], refs[23:27], refs[27:31], refs[31]
    q_all, d_all, k_own, v_own, d_key, d_value, sems = refs[32:39]
    copies = []
    for k in range(4):
        at = pl.ds(pl.multiple_of(block_of(idx, k) * ROWS, ROWS), ROWS)
        copies.append(pltpu.make_async_copy(k_hbm.at[at, :], k_own.at[k], sems.at[k]))
        copies.append(pltpu.make_async_copy(v_hbm.at[at, :], v_own.at[k], sems.at[k + 4]))
    copy_all(copies)
    hist = Histories(len_ref, tgt_ref)
    assemble(idx, q_pieces, [(q_all, 0)])
    assemble(idx, d_pieces, [(d_all, 0)])
    d_key[...] = jnp.zeros_like(d_key)
    d_value[...] = jnp.zeros_like(d_value)
    row = lax.broadcasted_iota(jnp.int32, (ROWS, TILE), 0)
    lane = lax.broadcasted_iota(jnp.int32, (1, TILE), 1)
    lows, highs = [], []
    for k in range(4):
        first = block_of(idx, k) * ROWS
        lows.append(first // TILE)
        highs.append((hist.pick(hist.ends, first + ROWS - 1) - 1) // TILE)
    for copy in copies:
        copy.wait()

    def body(k, t, valid):
        at = tile_at(t)
        queries, d_att = q_all[at, :], d_all[at, :]
        half = dot_t(k_own[k], queries) * (0.5 * DH**-0.5)
        d_attn = dot_t(v_own[k], d_att)
        key = block_of(idx, k) * ROWS + row
        pos = lane + t * TILE
        start, limit = hist.range_of(pos)
        start = start + jnp.where(valid, 0, TOKENS)
        seen = ((key >= start) & (key < limit)) | (key == pos)
        tanh = jnp.tanh(half)
        more = 1.0 + tanh
        weight = jnp.where(seen, half * more, 0.0).astype(bf16)
        factor = (SLOPE_SCALE * more) * (1.0 + half * (1.0 - tanh))
        d_raw = jnp.where(seen, d_attn * factor, 0.0).astype(bf16)
        d_key[k] += dot(d_raw, queries)
        d_value[k] += dot(weight, d_att)

    for_items(lows, highs, body)
    for k in range(4):
        d_q = dq_refs[k][...]
        d_k = (d_key[k] * SLOPE_REST * slope_ref[k, :, DH : 2 * DH]).astype(bf16)
        d_v = (d_value[k] * (1.0 / DIVISOR) * slope_ref[k, :, 2 * DH : 3 * DH]).astype(bf16)
        back_refs[k][:, 0:DH] = d_v
        back_refs[k][:, DH : 2 * DH] = d_q
        back_refs[k][:, 2 * DH : 3 * DH] = d_k
        at = pl.ds(k * ROWS, ROWS)
        all_ref[at, 0:DH] = d_refs[k][:, DH : 2 * DH]
        all_ref[at, DH : 2 * DH] = d_v
        all_ref[at, 2 * DH : 3 * DH] = d_q
        all_ref[at, 3 * DH : 4 * DH] = d_k


def key_grads(idx, lengths, targets, q_pieces, d_pieces, k_all, v_all, slope, d_query, d_att):
    return pl.pallas_call(
        key_kernel,
        in_specs=[SMEM] * 3 + [VMEM] * 16 + [HBM] * 2 + [VMEM] * 9,
        out_specs=[VMEM] * 5,
        out_shape=[shape((ROWS, 3 * DH), bf16)] * 4 + [shape((4 * ROWS, 4 * DH), bf16)],
        scratch_shapes=[pltpu.VMEM((TOKENS, DH), bf16)] * 2
        + [pltpu.VMEM((4, ROWS, DH), bf16)] * 2
        + [pltpu.VMEM((4, ROWS, DH), f32)] * 2
        + [pltpu.SemaphoreType.DMA((8,))],
        compiler_params=PARAMS,
        cost_estimate=cost(5),
        name="key_grads",
    )(idx, lengths, targets, *q_pieces, *d_pieces, k_all, v_all, slope, *d_query, *d_att)


def dot_first(a, b):
    return lax.dot_general(a, b, (((0,), (0,)), ((), ())), preferred_element_type=f32)


def parts_kernel(idx, own, got, o0, o1, o2, o3, rows, work):
    rows[0:ROWS, :] = own[0:ROWS, :]
    rows[ROWS : 2 * ROWS, :] = got[0:ROWS, :]
    for x in range(4):
        part = dot_first(rows[:, x * 128 : (x + 1) * 128], rows[:, 512:1536])
        score = dot_first(rows[:, 1536 + x * 256 : 1792 + x * 256], rows[:, 2560:2816])
        for c in range(2):

            @pl.when(idx[2] == c)
            def _(c=c, x=x, part=part, score=score):
                for y in range(4):
                    first, n = (x * 4 + y) * 24, y * 2 + c
                    work[first : first + 16, :] = part[n * 16 : (n + 1) * 16]
                    for j in range(4):
                        work[first + 16 : first + 24, j * 256 : (j + 1) * 256] = score[
                            n * 32 + j * 8 : n * 32 + (j + 1) * 8
                        ]

    head = [head_of(ref[ROWS : ROWS + 16, 0:512].astype(f32), 0) for ref in (own, got)]
    for k, ref in enumerate((o0, o1, o2, o3)):
        at = pl.ds(pl.multiple_of(lax.rem(idx[0] + k, 4) * 96, 8), 96)
        ref[...] = with_head(work[at, :], head[0] + head[1], 16)


def parts(idx, own, got):
    return pl.pallas_call(
        parts_kernel,
        in_specs=[SMEM] + [VMEM] * 2,
        out_specs=[VMEM] * 4,
        out_shape=[shape((112, 1024), bf16)] * 4,
        scratch_shapes=[pltpu.VMEM((2 * ROWS, ACTS), bf16), pltpu.VMEM((384, 1024), f32)],
        compiler_params=PARAMS,
        cost_estimate=cost(2),
        name="parts",
    )(idx, own, got)


def four(refs, pick):
    v = [pick(ref[...].astype(f32)) for ref in refs]
    return (v[0] + v[2]) + (v[1] + v[3])


def x_kernel(idx, e0, e1, e2, e3, *refs):
    outs, work = refs[0:4], refs[4]
    work[...] = four((e0, e1, e2, e3), lambda v: v)
    head = four((e0, e1, e2, e3), lambda v: head_of(v, 96))
    for k, ref in enumerate(outs):
        at = pl.ds(pl.multiple_of(lax.rem(idx[1] + k, 4) * 24, 8), 24)
        ref[...] = with_head(work[at, :], head, 8)


def x_sum(idx, early):
    return pl.pallas_call(
        x_kernel,
        in_specs=[SMEM] + [VMEM] * 4,
        out_specs=[VMEM] * 4,
        out_shape=[shape((32, 1024), bf16)] * 4,
        scratch_shapes=[pltpu.VMEM((112, 1024), f32)],
        compiler_params=PARAMS,
        cost_estimate=cost(1),
        name="x_sum",
    )(idx, *early)


def pack_kernel(in_ref, e0, e1, e2, e3, out_ref):
    for t in range(4):
        for h in range(HEADS):
            total = jnp.zeros((32, DH), f32)
            for n in range(8):
                total = total + in_ref[h * 8 + n, :, t * DH : (t + 1) * DH].astype(f32)
            z, half = divmod(t * HEADS + h, 2)
            out_ref[z, half * 32 : (half + 1) * 32, :] = total.astype(bf16)
    early = four((e0, e1, e2, e3), lambda v: v)
    high, low = two_of(four((e0, e1, e2, e3), lambda v: head_of(v, 24)))
    head = [high[:, 0:128], high[:, 128:256], low[:, 0:128], low[:, 128:256]]
    head = jnp.concatenate(head + [jnp.zeros((4, 128), f32)], axis=0)
    for z in range(8):
        score = [early[16:24, j * 256 + z * 32 : j * 256 + (z + 1) * 32] for j in range(4)]
        rows = [early[0:16, z * 128 : (z + 1) * 128], jnp.concatenate(score, axis=1), head]
        out_ref[z, 64:96, :] = jnp.concatenate(rows, axis=0).astype(bf16)


def pack(in_part, early):
    return pl.pallas_call(
        pack_kernel,
        in_specs=[VMEM] * 5,
        out_specs=VMEM,
        out_shape=shape((8, 96, 128), bf16),
        compiler_params=PARAMS,
        cost_estimate=cost(2),
        name="pack",
    )(in_part, *early)


def last_kernel(ref, in_ref, out_ref, score_ref, head_ref):
    total = ref[0].astype(f32)
    for z in range(1, 8):
        total = total + ref[z].astype(f32)
    in_ref[:, 0:128] = total[0:32]
    in_ref[:, 128:256] = total[32:64]
    out_ref[...] = total[64:80]
    for j in range(4):
        score_ref[j * 8 : (j + 1) * 8, :] = total[80:88, j * 32 : (j + 1) * 32]
    head_ref[:, 0:128] = total[88:89] + total[90:91]
    head_ref[:, 128:256] = total[89:90] + total[91:92]


def last_sum(value):
    return pl.pallas_call(
        last_kernel,
        in_specs=[VMEM],
        out_specs=[VMEM] * 4,
        out_shape=[
            shape((32, 256), f32),
            shape((16, 128), f32),
            shape((32, 32), f32),
            shape((1, 256), f32),
        ],
        compiler_params=PARAMS,
        cost_estimate=cost(1),
        name="last_sum",
    )(value)


def input_kernel(idx, b0, b1, b2, b3, gate_ref, w_ref, x_ref, grad, d_mid, w_score, out_ref, d_pre, d_norm):
    step = pl.program_id(0)
    width = HEADS * DH

    @pl.when(step == 0)
    def _():
        d_pre[:, 0:width] = gate_ref[...]
        for k, ref in enumerate((b0, b1, b2, b3)):
            head = lax.rem(idx[0] + k, 4)
            for kind in range(3):
                at = pl.ds(pl.multiple_of((kind + 1) * width + head * DH, DH), DH)
                d_pre[:, at] = ref[:, kind * DH : (kind + 1) * DH]

    d_norm[:, pl.ds(pl.multiple_of(step * 256, 256), 256)] = dot_t(d_pre[...], w_ref[...])

    @pl.when(step == 3)
    def _():
        normed, inverse = norm_rows(x_ref[...].astype(f32))
        d_total = grad[...].astype(f32) + dot_t(d_mid[...], w_score[...])
        out_ref[...] = (d_total + norm_back(d_norm[...], normed, inverse)).astype(bf16)


def input_grads(idx, back, gate, w_in, x, grad, d_mid, w_score):
    whole = lambda dims: pl.BlockSpec(dims, lambda i: (0, 0))
    return pl.pallas_call(
        input_kernel,
        grid=(4,),
        in_specs=[SMEM]
        + [whole((ROWS, 3 * DH))] * 4
        + [
            whole((ROWS, HEADS * DH)),
            pl.BlockSpec((256, 2048), lambda i: (i, 0)),
            whole((ROWS, 1024)),
            whole((ROWS, 1024)),
            whole((ROWS, 256)),
            whole((1024, 256)),
        ],
        out_specs=whole((ROWS, 1024)),
        out_shape=shape((ROWS, 1024), bf16),
        scratch_shapes=[pltpu.VMEM((ROWS, 2048), bf16), pltpu.VMEM((ROWS, 1024), f32)],
        compiler_params=PARAMS,
        cost_estimate=cost(4),
        name="input_grads",
    )(idx, *back, gate, w_in, x, grad, d_mid, w_score)


def join_kernel(columns, *refs):
    for i, column in enumerate(columns):
        for k in range(4):
            refs[-1][k, :, i * DH : (i + 1) * DH] = refs[4 * i + k][:, column : column + DH]


def join(parts_of):
    return pl.pallas_call(
        functools.partial(join_kernel, [column for _, column in parts_of]),
        in_specs=[VMEM] * 4 * len(parts_of),
        out_specs=VMEM,
        out_shape=shape((4, ROWS, DH * len(parts_of)), bf16),
        compiler_params=PARAMS,
        cost_estimate=cost(0.3),
        name="join",
    )(*[array for arrays, _ in parts_of for array in arrays])


def shifted(value, axis, by):
    size = lax.axis_size(axis)
    return lax.ppermute(value, axis, [(i, (i + by) % size) for i in range(size)])


def swapped(value, axis, bit):
    return lax.ppermute(value, axis, [(i, i ^ bit) for i in range(lax.axis_size(axis))])


def after(value, other):
    return lax.optimization_barrier((value, other))[0]


def exchange(values, sign):
    return [values[0]] + [shifted(values[k], "x", sign * k) for k in range(1, 4)]


def gathered(value, first=None):
    own = [value] + [shifted(value, "y", k) for k in range(1, 4)]
    other = swapped(value, "core", 1)
    late = own[1:] if first is None else after(own[1:], first())
    return own[0:1] + late + [other] + [swapped(piece, "core", 1) for piece in late]


def on_device(x_rows, lengths, targets, w_in, w_out, w_score, head_score, grad_out, grad_score):
    x, lengths, targets = x_rows[0], lengths[0], targets[0]
    idx = jnp.stack([lax.axis_index(a) for a in SEQ]).astype(jnp.int32)
    normed, kvq = project(idx, x, w_in)
    kvq = exchange(kvq, 1)
    kv_pieces = gathered(join([(kvq, 0), (kvq, DH)]))
    normed_all = exchange([after(normed, kvq[3])] * 4, 1)
    forwarded = forward(idx, lengths, targets, kvq, kv_pieces)
    k_all, v_all = forwarded[4:6]
    attended = exchange(forwarded[0:4], -1)
    slope = slopes(idx, after(normed_all, forwarded[0]), w_in)
    gate, gate_slope = gates(after(normed, slope), w_in)
    q_own = after(join([(kvq, 2 * DH)]), slope)
    q_got = [shifted(q_own, "y", k) for k in range(1, 4)]
    attended = after(attended, gate)
    mid = middle(
        idx, lengths, targets, attended, gate, gate_slope, x, w_out, w_score,
        head_score[None, :], grad_out[0], grad_score.reshape(ROWS, 1),
    )
    gate_full, acts, d_mid = mid[4:7]
    d_att = exchange(mid[0:4], 1)
    q_pieces = [q_own] + after(q_got, mid[0])
    q_pieces = q_pieces + [swapped(piece, "core", 1) for piece in q_pieces]
    early = parts(idx, acts, swapped(acts, "core", 1))
    d_own, q_pieces, early = lax.optimization_barrier((join([(d_att, 0)]), q_pieces, early))
    early = exchange(early, 1)
    d_query = query_grads(idx, lengths, targets, kvq, d_att, k_all, v_all, slope)
    d_pieces = gathered(d_own, lambda: d_query[0])
    d_query = after(d_query, early)
    keyed = key_grads(
        idx, lengths, targets, q_pieces, d_pieces, k_all, v_all, slope, d_query, d_att
    )
    back = exchange(keyed[0:4], -1)
    early = x_sum(idx, after(early, keyed[4]))
    early = [early[0]] + [shifted(early[k], "y", k) for k in range(1, 4)]
    in_part = dot_first(jnp.concatenate(normed_all, axis=0), keyed[4])
    in_part = lax.all_to_all(in_part.astype(bf16), SEQ, 0, 0, tiled=True).reshape(32, 32, 512)
    d_x = input_grads(idx, back, gate_full, w_in, x, grad_out[0], d_mid, w_score)
    last = lax.all_to_all(pack(in_part, early), "dp", 0, 0, tiled=True)
    d_w_in, d_w_out, d_w_score, d_head = last_sum(last)
    return d_x[None], d_w_in, d_w_out, d_w_score, d_head.reshape(256)


def solution(mesh):
    inner = Mesh(mesh.devices.reshape(8, 4, 4, 2), ("dp", "x", "y", "core"))
    placed = (
        P("dp", SEQ, None),
        P("dp", None),
        P("dp", None),
        P(),
        P(),
        P(),
        P(),
        P("dp", SEQ, None),
        P("dp", SEQ),
    )
    return jax.shard_map(
        on_device,
        mesh=inner,
        in_specs=placed,
        out_specs=(P("dp", SEQ, None), P(SEQ, "dp"), P(SEQ, "dp"), P(SEQ, "dp"), P()),
        check_vma=False,
    )
```

```python
import functools

import jax
import jax.numpy as jnp
from jax import lax
from jax.experimental import pallas as pl
from jax.experimental.pallas import tpu as pltpu
from jax.sharding import Mesh
from jax.sharding import PartitionSpec as P

HEADS = 4
DH = 128
ROWS = 128
HIST = 8
TOKENS = 4096
DIVISOR = 2048.0
TILE = 256
PAIR = 4
NORM_EPS = 1e-05
SEQ = ("x", "y", "core")

f32 = jnp.float32
bf16 = jnp.bfloat16
VMEM = pl.BlockSpec(memory_space=pltpu.VMEM)
SMEM = pl.BlockSpec(memory_space=pltpu.SMEM)
HBM = pl.BlockSpec(memory_space=pltpu.HBM)
PARAMS = pltpu.CompilerParams(vmem_limit_bytes=16 * 1024 * 1024)


def cost(us):
    return pl.CostEstimate(flops=int(us * 1.15e9), bytes_accessed=0, transcendentals=0)


def shape(dims, kind):
    return jax.ShapeDtypeStruct(dims, kind)


def dot(a, b):
    return lax.dot_general(a, b, (((1,), (0,)), ((), ())), preferred_element_type=f32)


def dot_t(a, b):
    return lax.dot_general(a, b, (((1,), (1,)), ((), ())), preferred_element_type=f32)


def sigmoid(value):
    return 0.5 + 0.5 * jnp.tanh(0.5 * value)


def silu_slope(value):
    sigma = sigmoid(value)
    return sigma * (1.0 + value * (1.0 - sigma))


def norm_rows(value):
    centre = value - jnp.mean(value, axis=-1, keepdims=True)
    inverse = lax.rsqrt(jnp.mean(centre * centre, axis=-1, keepdims=True) + NORM_EPS)
    return centre * inverse, inverse


def norm_back(grad, normed, inverse):
    return inverse * (
        grad
        - jnp.mean(grad, axis=-1, keepdims=True)
        - normed * jnp.mean(grad * normed, axis=-1, keepdims=True)
    )


class Histories:
    def __init__(self, len_ref, tgt_ref):
        self.starts, self.ends, self.firsts = [], [], []
        total = jnp.int32(0)
        for h in range(HIST):
            length = len_ref[h]
            self.starts.append(total)
            total = total + length
            self.ends.append(total)
            self.firsts.append(total - jnp.minimum(tgt_ref[h], length - 1))

    def pick(self, values, pos):
        out = jnp.where(pos >= self.starts[1], values[1], values[0])
        for h in range(2, HIST):
            out = jnp.where(pos >= self.starts[h], values[h], out)
        return out

    def range_of(self, pos):
        return self.pick(self.starts, pos), jnp.minimum(self.pick(self.firsts, pos), pos + 1)


def copy_all(copies):
    for copy in copies:
        copy.start()
    return copies


def project_kernel(x_hbm, w_hbm, normed_ref, o0, o1, o2, o3, x_ref, w_ref, sems):
    width = HEADS * DH
    copies = copy_all(
        [pltpu.make_async_copy(x_hbm, x_ref, sems.at[3])]
        + [
            pltpu.make_async_copy(w_hbm.at[:, pl.ds(kind * width, width)], w_ref.at[i], sems.at[i])
            for i, kind in enumerate((3, 1, 2))
        ]
    )
    copies[0].wait()
    value, _ = norm_rows(x_ref[...].astype(f32))
    normed = value.astype(bf16)
    normed_ref[...] = normed
    for i in range(3):
        copies[i + 1].wait()
        pre = dot(normed, w_ref[i])
        hidden = (pre * sigmoid(pre)).astype(bf16)
        for h in range(HEADS):
            away = lax.rem(h - lax.axis_index("x") + HEADS, HEADS)
            for k, ref in enumerate((o0, o1, o2, o3)):

                @pl.when(away == k)
                def _(ref=ref, h=h):
                    ref[:, i * DH : (i + 1) * DH] = hidden[:, h * DH : (h + 1) * DH]


def project(x, w_in):
    out = pl.pallas_call(
        project_kernel,
        in_specs=[HBM, HBM],
        out_specs=[VMEM] * 5,
        out_shape=[shape((ROWS, 1024), bf16)] + [shape((ROWS, 3 * DH), bf16)] * 4,
        scratch_shapes=[
            pltpu.VMEM((ROWS, 1024), bf16),
            pltpu.VMEM((3, 1024, HEADS * DH), bf16),
            pltpu.SemaphoreType.DMA((4,)),
        ],
        compiler_params=pltpu.CompilerParams(vmem_limit_bytes=60 * 1024 * 1024),
        cost_estimate=cost(3),
        name="project",
    )(x, w_in)
    return out[0], out[1:5]


def gates_kernel(normed_ref, w_hbm, gate_ref, slope_ref, w_ref, sem):
    copy = pltpu.make_async_copy(w_hbm.at[:, pl.ds(0, HEADS * DH)], w_ref, sem)
    copy.start()
    copy.wait()
    pre = dot(normed_ref[...], w_ref[...])
    sigma = sigmoid(pre)
    gate_ref[...] = (pre * sigma).astype(bf16)
    slope_ref[...] = sigma * (1.0 + pre * (1.0 - sigma))


def gates(normed, w_in):
    width = HEADS * DH
    return pl.pallas_call(
        gates_kernel,
        in_specs=[VMEM, HBM],
        out_specs=[VMEM] * 2,
        out_shape=[shape((ROWS, width), bf16), shape((ROWS, width), f32)],
        scratch_shapes=[pltpu.VMEM((1024, width), bf16), pltpu.SemaphoreType.DMA],
        compiler_params=PARAMS,
        cost_estimate=cost(0.2),
        name="gates",
    )(normed, w_in)


def slopes_kernel(idx, n0, n1, n2, n3, w_hbm, out_ref, w_ref, sems):
    copies = []
    for i, kind in enumerate((2, 3, 1)):
        at = pl.ds(pl.multiple_of((kind * HEADS + idx[0]) * DH, DH), DH)
        copies.append(pltpu.make_async_copy(w_hbm.at[:, at], w_ref.at[i], sems.at[i]))
    copy_all(copies)
    for i in range(3):
        copies[i].wait()
        for k, ref in enumerate((n0, n1, n2, n3)):
            out_ref[k, :, i * DH : (i + 1) * DH] = silu_slope(dot(ref[...], w_ref[i]))


def slopes(idx, normed, w_in):
    return pl.pallas_call(
        slopes_kernel,
        in_specs=[SMEM] + [VMEM] * 4 + [HBM],
        out_specs=VMEM,
        out_shape=shape((4, ROWS, 3 * DH), f32),
        scratch_shapes=[pltpu.VMEM((3, 1024, DH), bf16), pltpu.SemaphoreType.DMA((3,))],
        compiler_params=PARAMS,
        cost_estimate=cost(0.5),
        name="slopes",
    )(idx, *normed, w_in)


def block_of(idx, k):
    return lax.rem(idx[0] - k + 4, 4) * 8 + idx[1] * 2 + idx[2]


WHOLE = [(j % 4, j // 4, 0, 4) for j in range(8)]
NEAR = [(0, 0, 0, 4), (1, 0, 0, 4), (3, 0, 0, 4), (0, 1, 0, 4), (1, 1, 0, 4), (3, 1, 0, 4)]


def assemble(idx, pieces, places, outs):
    for piece, (back, other, first, count) in zip(pieces, places, strict=True):
        at_y = lax.rem(idx[1] - back + 4, 4)
        at_core = 1 - idx[2] if other else idx[2]
        for i in range(count):
            block = lax.rem(idx[0] - first - i + 4, 4) * 8 + at_y * 2 + at_core
            where = pl.ds(pl.multiple_of(block * ROWS, ROWS), ROWS)
            for ref, column in outs:
                ref[where, :] = piece[i, :, column : column + DH]


def for_items(lows, highs, body):
    ends, total = [], jnp.int32(0)
    for low, high in zip(lows, highs, strict=True):
        total = total + (high - low + 1)
        ends.append(total)

    def step(i, carry):
        for j in range(PAIR):
            n = i * PAIR + j
            k, t = jnp.int32(0), n + lows[0]
            for q in range(1, 4):
                k = jnp.where(n >= ends[q - 1], q, k)
                t = jnp.where(n >= ends[q - 1], n - ends[q - 1] + lows[q], t)
            body(k, t, n < total)
        return carry

    lax.fori_loop(0, (total + PAIR - 1) // PAIR, step, 0)


def tile_at(t):
    return pl.ds(pl.multiple_of(jnp.minimum(t, TOKENS // TILE - 1) * TILE, TILE), TILE)


def set_marks(idx, hist, marks):
    row = lax.broadcasted_iota(jnp.int32, (ROWS, 128), 0)
    lows, highs = [], []
    for k in range(4):
        first = block_of(idx, k) * ROWS
        start, limit = hist.range_of(first + row)
        marks[0, k], marks[1, k] = start, limit
        lows.append(hist.pick(hist.starts, first) // TILE)
        highs.append(first // TILE)
    return lows, highs


def seen_by(idx, marks, k, t):
    row = lax.broadcasted_iota(jnp.int32, (ROWS, TILE), 0)
    lane = lax.broadcasted_iota(jnp.int32, (ROWS, TILE), 1)
    key = lane + t * TILE
    start, limit = [jnp.concatenate([marks[i, k]] * (TILE // 128), axis=1) for i in range(2)]
    return ((key >= start) & (key < limit)) | (key - row == block_of(idx, k) * ROWS)


def attend(idx, marks, q_own, total, k, t, keys, values):
    half = dot_t(q_own[k], keys) * (0.5 * DH**-0.5)
    weight = half * (1.0 + jnp.tanh(half))
    weight = jnp.where(seen_by(idx, marks, k, t), weight, 0.0).astype(bf16)
    total[k] += dot(weight, values)


def near_kernel(idx, len_ref, tgt_ref, *refs):
    pieces, out, all_hbm = refs[0:6], refs[6], refs[7:10]
    k_all, v_all, q_all, q_own, marks, sems = refs[10:16]
    hist = Histories(len_ref, tgt_ref)
    for x in range(4):
        at = pl.ds(pl.multiple_of((x * 4 + lax.rem(idx[1] + 2, 4)) * TILE, TILE), TILE)
        for ref in (k_all, v_all, q_all):
            ref[at, :] = jnp.zeros((TILE, DH), bf16)
    assemble(idx, pieces, NEAR, [(k_all, 0), (v_all, DH), (q_all, 2 * DH)])
    copies = copy_all(
        [
            pltpu.make_async_copy(ref, all_hbm[i], sems.at[i])
            for i, ref in enumerate((k_all, v_all, q_all))
        ]
    )
    for k in range(4):
        q_own[k] = pieces[0][k, :, 2 * DH : 3 * DH]
    out[...] = jnp.zeros_like(out)
    lows, highs = set_marks(idx, hist, marks)
    base = 3 - lax.rem(idx[1] + 2, 4)
    lows = [(low + base) // 4 * 3 + jnp.minimum((low + base) % 4, 3) for low in lows]
    highs = [(high + base) // 4 * 3 + jnp.minimum((high + base) % 4, 2) for high in highs]

    def body(k, u, valid):
        t = u + u // 3 - base
        at = tile_at(t)
        attend(idx, marks, q_own, out, k, t, k_all[at, :], v_all[at, :])

    for_items(lows, highs, body)
    for copy in copies:
        copy.wait()


def attend_near(idx, lengths, targets, pieces):
    return pl.pallas_call(
        near_kernel,
        in_specs=[SMEM] * 3 + [VMEM] * 6,
        out_specs=[VMEM] + [HBM] * 3,
        out_shape=[shape((4, ROWS, DH), f32)] + [shape((TOKENS, DH), bf16)] * 3,
        scratch_shapes=[pltpu.VMEM((TOKENS, DH), bf16)] * 3
        + [
            pltpu.VMEM((4, ROWS, DH), bf16),
            pltpu.VMEM((2, 4, ROWS, 128), jnp.int32),
            pltpu.SemaphoreType.DMA((3,)),
        ],
        compiler_params=PARAMS,
        cost_estimate=cost(0.5),
        name="attend_near",
    )(idx, lengths, targets, *pieces)


def far_kernel(idx, len_ref, tgt_ref, *refs):
    held, pieces, near, o_refs, all_hbm = refs[0], refs[1:5], refs[5], refs[9:13], refs[13:16]
    k_far, v_far, q_far, q_own, total, marks, sems = refs[16:23]
    hist = Histories(len_ref, tgt_ref)
    far = lax.rem(idx[1] + 2, 4)
    for j in range(4):
        other, first = j // 2, j % 2 * 2
        at_core = 1 - idx[2] if other else idx[2]
        for i in range(2):
            x = lax.rem(idx[0] - first - i + 4, 4)
            where = pl.ds(pl.multiple_of(x * TILE + at_core * ROWS, ROWS), ROWS)
            for n, ref in enumerate((k_far, v_far, q_far)):
                ref[where, :] = pieces[j][i, :, n * DH : (n + 1) * DH]
    copies = []
    for x in range(4):
        at = pl.ds(pl.multiple_of((x * 4 + far) * TILE, TILE), TILE)
        for n, ref in enumerate((k_far, v_far, q_far)):
            tile = ref.at[x * TILE : (x + 1) * TILE, :]
            copies.append(pltpu.make_async_copy(tile, all_hbm[n].at[at, :], sems.at[x * 3 + n]))
    copy_all(copies)
    for k in range(4):
        q_own[k] = held[k, :, 2 * DH : 3 * DH]
    total[...] = near[...]
    lows, highs = set_marks(idx, hist, marks)
    lows = [(low - far + 3) // 4 for low in lows]
    highs = [(high - far + 4) // 4 - 1 for high in highs]

    def body(k, u, valid):
        at = pl.ds(pl.multiple_of(jnp.minimum(u, 3) * TILE, TILE), TILE)
        attend(idx, marks, q_own, total, k, u * 4 + far, k_far[at, :], v_far[at, :])

    for_items(lows, highs, body)
    for k in range(4):
        o_refs[k][...] = total[k] * (1.0 / DIVISOR)
    for copy in copies:
        copy.wait()


def attend_far(idx, lengths, targets, held, pieces, near, everything):
    return pl.pallas_call(
        far_kernel,
        in_specs=[SMEM] * 3 + [VMEM] * 6 + [HBM] * 3,
        out_specs=[VMEM] * 4 + [HBM] * 3,
        out_shape=[shape((ROWS, DH), f32)] * 4 + [shape((TOKENS, DH), bf16)] * 3,
        input_output_aliases={9: 4, 10: 5, 11: 6},
        scratch_shapes=[pltpu.VMEM((4 * TILE, DH), bf16)] * 3
        + [
            pltpu.VMEM((4, ROWS, DH), bf16),
            pltpu.VMEM((4, ROWS, DH), f32),
            pltpu.VMEM((2, 4, ROWS, 128), jnp.int32),
            pltpu.SemaphoreType.DMA((12,)),
        ],
        compiler_params=PARAMS,
        cost_estimate=cost(0.5),
        name="attend_far",
    )(idx, lengths, targets, held, *pieces, near, *everything)


def two_of(head):
    high = head.astype(bf16).astype(f32)
    return high, (head - high).astype(bf16).astype(f32)


def with_head(rows, head, count):
    high, low = two_of(head)
    width = ACTS if rows is None else rows.shape[1]
    line = jnp.concatenate([high, low, jnp.zeros((1, width - 512), f32)], axis=1)
    line = jnp.concatenate([line, jnp.zeros((count - 1, width), f32)], axis=0)
    return (line if rows is None else jnp.concatenate([rows, line], axis=0)).astype(bf16)


def head_of(value, row):
    return value[row : row + 1, 0:256] + value[row : row + 1, 256:512]


ACTS = 512 + 1024 + 1024 + 256


def middle_kernel(idx, len_ref, tgt_ref, a0, a1, a2, a3, gate_ref, slope_ref, x_ref, w_out, w_score, head, grad, score, *refs):
    d_refs, g_full, acts, mid_ref = refs[0:4], refs[4], refs[5], refs[6]
    att, work = refs[7:9]
    for k, ref in enumerate((a0, a1, a2, a3)):
        at = pl.ds(pl.multiple_of(lax.rem(idx[0] + k, 4) * DH, DH), DH)
        att[:, at] = ref[...]
    onorm, inverse = norm_rows(att[...])
    gate = gate_ref[...].astype(f32)
    gated = (onorm * gate).astype(bf16)
    acts[0:ROWS, 0:512] = gated
    out_b = (x_ref[...].astype(f32) + dot(gated, w_out[...])).astype(bf16)
    acts[0:ROWS, 1536:2560] = out_b
    mid = dot(out_b, w_score[...])
    hist = Histories(len_ref, tgt_ref)
    own = ((idx[0] * 4 + idx[1]) * 2 + idx[2]) * ROWS
    pos = own + lax.broadcasted_iota(jnp.int32, (ROWS, 1), 0)
    diagonal = lax.broadcasted_iota(jnp.int32, (ROWS, ROWS), 0) == lax.broadcasted_iota(
        jnp.int32, (ROWS, ROWS), 1
    )
    column = jnp.sum(jnp.where(diagonal, score[...], 0.0), axis=1, keepdims=True)
    weight = jnp.where(pos >= hist.pick(hist.firsts, pos), column, 0.0)
    sigma = sigmoid(mid)
    head_part = jnp.sum(weight * (mid * sigma), axis=0, keepdims=True)
    acts[ROWS : ROWS + 16, :] = with_head(None, head_part, 16)
    d_mid = (weight * head[...] * (sigma * (1.0 + mid * (1.0 - sigma)))).astype(bf16)
    acts[0:ROWS, 2560:2816] = d_mid
    mid_ref[...] = d_mid
    total_b = (grad[...].astype(f32) + dot_t(d_mid, w_score[...])).astype(bf16)
    acts[0:ROWS, 512:1536] = total_b
    d_gated = dot_t(total_b, w_out[...])
    att[...] = norm_back(d_gated * gate, onorm, inverse)
    work[...] = d_gated * onorm * slope_ref[...]
    g_full[...] = work[...].astype(bf16)
    for k in range(4):
        at = pl.ds(pl.multiple_of(lax.rem(idx[0] + k, 4) * DH, DH), DH)
        d_refs[k][:, 0:DH] = att[:, at].astype(bf16)
        d_refs[k][:, DH : 2 * DH] = work[:, at].astype(bf16)


def middle(idx, lengths, targets, attended, gate, slope, x, w_out, w_score, head, grad, score):
    width = HEADS * DH
    return pl.pallas_call(
        middle_kernel,
        in_specs=[SMEM] * 3 + [VMEM] * 12,
        out_specs=[VMEM] * 7,
        out_shape=[shape((ROWS, 2 * DH), bf16)] * 4
        + [
            shape((ROWS, width), bf16),
            shape((ROWS + 16, ACTS), bf16),
            shape((ROWS, 256), bf16),
        ],
        scratch_shapes=[pltpu.VMEM((ROWS, width), f32)] * 2,
        compiler_params=PARAMS,
        cost_estimate=cost(0.5),
        name="middle",
    )(idx, lengths, targets, *attended, gate, slope, x, w_out, w_score, head, grad, score)


SLOPE_SCALE = 0.5 * 2**-0.5
SLOPE_REST = DH**-0.5 / DIVISOR / 2**-0.5


def query_kernel(idx, len_ref, tgt_ref, *refs):
    held, d_refs, (k_hbm, v_hbm), out_refs = refs[0], refs[1:5], refs[5:7], refs[7:11]
    k_all, v_all, q_own, d_own, total, marks, sems = refs[11:18]
    copies = copy_all(
        [
            pltpu.make_async_copy(k_hbm, k_all, sems.at[0]),
            pltpu.make_async_copy(v_hbm, v_all, sems.at[1]),
        ]
    )
    hist = Histories(len_ref, tgt_ref)
    for k in range(4):
        q_own[k] = held[k, :, 2 * DH : 3 * DH]
        d_own[k] = d_refs[k][:, 0:DH]
    total[...] = jnp.zeros_like(total)
    lows, highs = set_marks(idx, hist, marks)
    for copy in copies:
        copy.wait()

    def body(k, t, valid):
        at = tile_at(t)
        keys = k_all[at, :]
        half = dot_t(q_own[k], keys) * (0.5 * DH**-0.5)
        d_attn = dot_t(d_own[k], v_all[at, :])
        tanh = jnp.tanh(half)
        factor = (SLOPE_SCALE + SLOPE_SCALE * tanh) * (1.0 + half * (1.0 - tanh))
        d_raw = jnp.where(seen_by(idx, marks, k, t), d_attn * factor, 0.0).astype(bf16)
        total[k] += dot(d_raw, keys)

    for_items(lows, highs, body)
    for k in range(4):
        out_refs[k][...] = total[k] * SLOPE_REST


def query_grads(idx, lengths, targets, held, d_att, k_all, v_all):
    return pl.pallas_call(
        query_kernel,
        in_specs=[SMEM] * 3 + [VMEM] * 5 + [HBM] * 2,
        out_specs=[VMEM] * 4,
        out_shape=[shape((ROWS, DH), f32)] * 4,
        scratch_shapes=[pltpu.VMEM((TOKENS, DH), bf16)] * 2
        + [pltpu.VMEM((4, ROWS, DH), bf16)] * 2
        + [
            pltpu.VMEM((4, ROWS, DH), f32),
            pltpu.VMEM((2, 4, ROWS, 128), jnp.int32),
            pltpu.SemaphoreType.DMA((2,)),
        ],
        compiler_params=PARAMS,
        cost_estimate=cost(3),
        name="query_grads",
    )(idx, lengths, targets, held, *d_att, k_all, v_all)


def key_kernel(idx, len_ref, tgt_ref, *refs):
    d_pieces, (k_hbm, v_hbm, q_hbm, slope_ref) = refs[0:8], refs[8:12]
    dq_refs, d_refs, back_refs, all_ref = refs[12:16], refs[16:20], refs[20:24], refs[24]
    q_all, d_all, k_own, v_own, d_key, d_value, sems = refs[25:32]
    copies = [pltpu.make_async_copy(q_hbm, q_all, sems.at[8])]
    for k in range(4):
        at = pl.ds(pl.multiple_of(block_of(idx, k) * ROWS, ROWS), ROWS)
        copies.append(pltpu.make_async_copy(k_hbm.at[at, :], k_own.at[k], sems.at[k]))
        copies.append(pltpu.make_async_copy(v_hbm.at[at, :], v_own.at[k], sems.at[k + 4]))
    copy_all(copies)
    hist = Histories(len_ref, tgt_ref)
    assemble(idx, d_pieces, WHOLE, [(d_all, 0)])
    d_key[...] = jnp.zeros_like(d_key)
    d_value[...] = jnp.zeros_like(d_value)
    row = lax.broadcasted_iota(jnp.int32, (ROWS, TILE), 0)
    lane = lax.broadcasted_iota(jnp.int32, (1, TILE), 1)
    lows, highs = [], []
    for k in range(4):
        first = block_of(idx, k) * ROWS
        lows.append(first // TILE)
        highs.append((hist.pick(hist.ends, first + ROWS - 1) - 1) // TILE)
    for copy in copies:
        copy.wait()

    def body(k, t, valid):
        at = tile_at(t)
        queries, d_att = q_all[at, :], d_all[at, :]
        half = dot_t(k_own[k], queries) * (0.5 * DH**-0.5)
        d_attn = dot_t(v_own[k], d_att)
        key = block_of(idx, k) * ROWS + row
        pos = lane + t * TILE
        start, limit = hist.range_of(pos)
        start = start + jnp.where(valid, 0, TOKENS)
        seen = ((key >= start) & (key < limit)) | (key == pos)
        tanh = jnp.tanh(half)
        more = 1.0 + tanh
        weight = jnp.where(seen, half * more, 0.0).astype(bf16)
        factor = (SLOPE_SCALE * more) * (1.0 + half * (1.0 - tanh))
        d_raw = jnp.where(seen, d_attn * factor, 0.0).astype(bf16)
        d_key[k] += dot(d_raw, queries)
        d_value[k] += dot(weight, d_att)

    for_items(lows, highs, body)
    for k in range(4):
        d_q = (dq_refs[k][...] * slope_ref[k, :, 0:DH]).astype(bf16)
        d_k = (d_key[k] * SLOPE_REST * slope_ref[k, :, DH : 2 * DH]).astype(bf16)
        d_v = (d_value[k] * (1.0 / DIVISOR) * slope_ref[k, :, 2 * DH : 3 * DH]).astype(bf16)
        back_refs[k][:, 0:DH] = d_v
        back_refs[k][:, DH : 2 * DH] = d_q
        back_refs[k][:, 2 * DH : 3 * DH] = d_k
        at = pl.ds(k * ROWS, ROWS)
        all_ref[at, 0:DH] = d_refs[k][:, DH : 2 * DH]
        all_ref[at, DH : 2 * DH] = d_v
        all_ref[at, 2 * DH : 3 * DH] = d_q
        all_ref[at, 3 * DH : 4 * DH] = d_k


def key_grads(idx, lengths, targets, d_pieces, everything, slope, d_query, d_att):
    return pl.pallas_call(
        key_kernel,
        in_specs=[SMEM] * 3 + [VMEM] * 8 + [HBM] * 3 + [VMEM] * 9,
        out_specs=[VMEM] * 5,
        out_shape=[shape((ROWS, 3 * DH), bf16)] * 4 + [shape((4 * ROWS, 4 * DH), bf16)],
        scratch_shapes=[pltpu.VMEM((TOKENS, DH), bf16)] * 2
        + [pltpu.VMEM((4, ROWS, DH), bf16)] * 2
        + [pltpu.VMEM((4, ROWS, DH), f32)] * 2
        + [pltpu.SemaphoreType.DMA((9,))],
        compiler_params=PARAMS,
        cost_estimate=cost(0.02),
        name="key_grads",
    )(idx, lengths, targets, *d_pieces, *everything, slope, *d_query, *d_att)


def dot_first(a, b):
    return lax.dot_general(a, b, (((0,), (0,)), ((), ())), preferred_element_type=f32)


def parts_kernel(idx, own, got, out, rows):
    rows[0:ROWS, :] = own[0:ROWS, :]
    rows[ROWS : 2 * ROWS, :] = got[0:ROWS, :]
    total = rows[:, pl.ds(pl.multiple_of(512 + idx[2] * 512, 512), 512)]
    d_mid = rows[:, pl.ds(pl.multiple_of(2560 + idx[2] * 128, 128), 128)]
    head = [head_of(ref[ROWS : ROWS + 16, 0:512].astype(f32), 0) for ref in (own, got)]
    high, low = two_of(head[0] + head[1])
    line = jnp.concatenate([high, low], axis=1)
    line = jnp.concatenate([line, jnp.zeros((7, 512), f32)], axis=0)
    for x in range(4):
        part = dot_first(rows[:, x * 128 : (x + 1) * 128], total)
        score = dot_first(rows[:, 1536 + x * 256 : 1792 + x * 256], d_mid)
        for m in range(8):
            last = [score[m * 32 + j * 8 : m * 32 + (j + 1) * 8] for j in range(4)]
            block = [part[m * 16 : (m + 1) * 16], jnp.concatenate(last, axis=1), line]
            out[x * 8 + m] = jnp.concatenate(block, axis=0).astype(bf16)


def parts(idx, own, got):
    return pl.pallas_call(
        parts_kernel,
        in_specs=[SMEM] + [VMEM] * 2,
        out_specs=VMEM,
        out_shape=shape((32, 32, 512), bf16),
        scratch_shapes=[pltpu.VMEM((2 * ROWS, ACTS), bf16)],
        compiler_params=PARAMS,
        cost_estimate=cost(0.3),
        name="parts",
    )(idx, own, got)


def weights_kernel(idx, n0, n1, n2, n3, d_pre, keep, send, left):
    for k, ref in enumerate((n0, n1, n2, n3)):
        left[k * ROWS : (k + 1) * ROWS, :] = ref[...]
    for n in range(4):
        part = dot_first(left[:, n * 256 : (n + 1) * 256], d_pre[...])
        for c in range(2):

            @pl.when(idx[2] == c)
            def _(c=c, n=n, part=part):
                for i in range(8):
                    rows = [part[i * 32 : i * 32 + 16], part[i * 32 + 16 : (i + 1) * 32]]
                    halves_of = [
                        jnp.concatenate([v[:, d * 256 : (d + 1) * 256] for v in rows], axis=1)
                        for d in (c, 1 - c)
                    ]
                    keep[n * 8 + i] = halves_of[0]
                    send[n * 8 + i] = halves_of[1].astype(bf16)


def weights(idx, normed, d_pre):
    return pl.pallas_call(
        weights_kernel,
        in_specs=[SMEM] + [VMEM] * 5,
        out_specs=[VMEM] * 2,
        out_shape=[shape((32, 16, 512), f32), shape((32, 16, 512), bf16)],
        scratch_shapes=[pltpu.VMEM((512, 1024), bf16)],
        compiler_params=PARAMS,
        cost_estimate=cost(0.02),
        name="weights",
    )(idx, *normed, d_pre)


def merge_kernel(keep, got, early, out):
    for n in range(32):
        out[n, 0:16, :] = (keep[n] + got[n].astype(f32)).astype(bf16)
        out[n, 16:48, :] = early[n]


def merge(keep, got, early):
    return pl.pallas_call(
        merge_kernel,
        in_specs=[VMEM] * 3,
        out_specs=VMEM,
        out_shape=shape((32, 48, 512), bf16),
        compiler_params=PARAMS,
        cost_estimate=cost(0.3),
        name="merge",
    )(keep, got, early)


def pack_kernel(ref, out_ref):
    for c in range(2):
        for h in range(HEADS):
            total = ref[h * 8 + c, 0:16, :].astype(f32)
            for n in range(1, 4):
                total = total + ref[h * 8 + n * 2 + c, 0:16, :].astype(f32)
            for i in range(2):
                z, half = divmod((c * 2 + i) * HEADS + h, 2)
                rows = [total[:, r * 256 + i * 128 : r * 256 + (i + 1) * 128] for r in range(2)]
                rows = jnp.concatenate(rows, axis=0).astype(bf16)
                out_ref[z, half * 32 : (half + 1) * 32, :] = rows
    sums = []
    for c in range(2):
        total = ref[c, 16:48, :].astype(f32)
        head = head_of(total, 24)
        for n in range(c + 2, 32, 2):
            part = ref[n, 16:48, :].astype(f32)
            total, head = total + part, head + head_of(part, 24)
        sums.append(total)
    high, low = two_of(head)
    head = [high[:, 0:128], high[:, 128:256], low[:, 0:128], low[:, 128:256]]
    head = jnp.concatenate(head + [jnp.zeros((4, 128), f32)], axis=0)
    for z in range(8):
        total, at = sums[z // 4], z % 4 * 128
        score = [total[16:24, j * 128 + z % 4 * 32 : j * 128 + z % 4 * 32 + 32] for j in range(4)]
        rows = [total[0:16, at : at + 128], jnp.concatenate(score, axis=1), head]
        out_ref[z, 64:96, :] = jnp.concatenate(rows, axis=0).astype(bf16)


def pack(value):
    return pl.pallas_call(
        pack_kernel,
        in_specs=[VMEM],
        out_specs=VMEM,
        out_shape=shape((8, 96, 128), bf16),
        compiler_params=PARAMS,
        cost_estimate=cost(0.3),
        name="pack",
    )(value)


def last_kernel(ref, in_ref, out_ref, score_ref, head_ref):
    total = ref[0].astype(f32)
    for z in range(1, 8):
        total = total + ref[z].astype(f32)
    in_ref[:, 0:128] = total[0:32]
    in_ref[:, 128:256] = total[32:64]
    out_ref[...] = total[64:80]
    for j in range(4):
        score_ref[j * 8 : (j + 1) * 8, :] = total[80:88, j * 32 : (j + 1) * 32]
    head_ref[:, 0:128] = total[88:89] + total[90:91]
    head_ref[:, 128:256] = total[89:90] + total[91:92]


def last_sum(value):
    return pl.pallas_call(
        last_kernel,
        in_specs=[VMEM],
        out_specs=[VMEM] * 4,
        out_shape=[
            shape((32, 256), f32),
            shape((16, 128), f32),
            shape((32, 32), f32),
            shape((1, 256), f32),
        ],
        compiler_params=PARAMS,
        cost_estimate=cost(0.3),
        name="last_sum",
    )(value)


def input_kernel(idx, b0, b1, b2, b3, gate_ref, w_ref, x_ref, grad, d_mid, w_score, out_ref, d_pre, d_norm):
    step = pl.program_id(0)
    width = HEADS * DH

    @pl.when(step == 0)
    def _():
        d_pre[:, 0:width] = gate_ref[...]
        for k, ref in enumerate((b0, b1, b2, b3)):
            head = lax.rem(idx[0] + k, 4)
            for kind in range(3):
                at = pl.ds(pl.multiple_of((kind + 1) * width + head * DH, DH), DH)
                d_pre[:, at] = ref[:, kind * DH : (kind + 1) * DH]

    d_norm[:, pl.ds(pl.multiple_of(step * 256, 256), 256)] = dot_t(d_pre[...], w_ref[...])

    @pl.when(step == 3)
    def _():
        normed, inverse = norm_rows(x_ref[...].astype(f32))
        d_total = grad[...].astype(f32) + dot_t(d_mid[...], w_score[...])
        out_ref[...] = (d_total + norm_back(d_norm[...], normed, inverse)).astype(bf16)


def input_grads(idx, back, gate, w_in, x, grad, d_mid, w_score):
    whole = lambda dims: pl.BlockSpec(dims, lambda i: (0, 0))
    return pl.pallas_call(
        input_kernel,
        grid=(4,),
        in_specs=[SMEM]
        + [whole((ROWS, 3 * DH))] * 4
        + [
            whole((ROWS, HEADS * DH)),
            pl.BlockSpec((256, 2048), lambda i: (i, 0)),
            whole((ROWS, 1024)),
            whole((ROWS, 1024)),
            whole((ROWS, 256)),
            whole((1024, 256)),
        ],
        out_specs=whole((ROWS, 1024)),
        out_shape=shape((ROWS, 1024), bf16),
        scratch_shapes=[pltpu.VMEM((ROWS, 2048), bf16), pltpu.VMEM((ROWS, 1024), f32)],
        compiler_params=PARAMS,
        cost_estimate=cost(1),
        name="input_grads",
    )(idx, *back, gate, w_in, x, grad, d_mid, w_score)


def join_kernel(*refs):
    for k in range(4):
        refs[4][k] = refs[k][:, 0 : refs[4].shape[2]]


def join(arrays, width):
    return pl.pallas_call(
        join_kernel,
        in_specs=[VMEM] * 4,
        out_specs=VMEM,
        out_shape=shape((4, ROWS, width), bf16),
        compiler_params=PARAMS,
        cost_estimate=cost(0.1),
        name="join",
    )(*arrays)


def halves_kernel(back, ahead, low, high):
    low[...] = back[0:2]
    high[...] = ahead[2:4]


def halves(back, ahead):
    return pl.pallas_call(
        halves_kernel,
        in_specs=[VMEM] * 2,
        out_specs=[VMEM] * 2,
        out_shape=[shape((2,) + back.shape[1:], bf16)] * 2,
        compiler_params=PARAMS,
        cost_estimate=cost(0.1),
        name="halves",
    )(back, ahead)


def shifted(value, axis, by):
    size = lax.axis_size(axis)
    return lax.ppermute(value, axis, [(i, (i + by) % size) for i in range(size)])


def swapped(value, axis, bit):
    return lax.ppermute(value, axis, [(i, i ^ bit) for i in range(lax.axis_size(axis))])


def after(value, other):
    return lax.optimization_barrier((value, other))[0]


def exchange(values, sign):
    return [values[0]] + [shifted(values[k], "x", sign * k) for k in range(1, 4)]


def with_core(pieces):
    return pieces + [swapped(piece, "core", 1) for piece in pieces]


def gathered_ring(value):
    near = [value, shifted(value, "y", 1), shifted(value, "y", -1)]
    low, high = halves(near[1], near[2])
    far = [shifted(low, "y", 1), shifted(high, "y", -1)]
    return with_core(near), far


def on_device(x_rows, lengths, targets, w_in, w_out, w_score, head_score, grad_out, grad_score):
    x, lengths, targets = x_rows[0], lengths[0], targets[0]
    idx = jnp.stack([lax.axis_index(a) for a in SEQ]).astype(jnp.int32)
    normed, kvq = project(x, w_in)
    kvq = exchange(kvq, 1)
    held = join(kvq, 3 * DH)
    near_pieces, far_pieces = gathered_ring(held)
    normed = after(normed, kvq[3])
    near = [shifted(normed, "x", 1), shifted(normed, "x", -1)]
    normed_all = [normed, near[0], shifted(after(normed, near), "x", 2), near[1]]
    partly = attend_near(idx, lengths, targets, near_pieces)
    far_pieces, near, partly = lax.optimization_barrier((far_pieces, near, partly))
    far_pieces = with_core(far_pieces)
    forwarded = attend_far(idx, lengths, targets, held, far_pieces, partly[0], partly[1:4])
    k_all, v_all, q_all = forwarded[4:7]
    attended = exchange(forwarded[0:4], -1)
    gate, gate_slope = gates(after(normed, forwarded[0]), w_in)
    slope = slopes(idx, after(normed_all, forwarded[0]), w_in)
    attended = after(attended, slope)
    mid = middle(
        idx, lengths, targets, attended, gate, gate_slope, x, w_out, w_score,
        head_score.reshape(1, 256), grad_out[0], grad_score,
    )
    gate_full, acts, d_mid = mid[4:7]
    d_att = exchange(mid[0:4], 1)
    acts_other = swapped(after(acts, d_att), "core", 1)
    d_own = join(d_att, DH)
    late = [shifted(d_own, "y", k) for k in range(1, 4)]
    d_query = query_grads(idx, lengths, targets, held, d_att, k_all, v_all)
    early = parts(idx, after(acts, d_query[0]), acts_other)
    d_pieces = with_core([d_own] + after(late, early))
    keyed = key_grads(
        idx, lengths, targets, d_pieces, (k_all, v_all, q_all), slope, d_query, d_att
    )
    keep, send = weights(idx, normed_all, keyed[4])
    got = swapped(send, "core", 1)
    partial = merge(keep, got, early)
    back, partial = lax.optimization_barrier((keyed[0:4], partial))
    partial = lax.all_to_all(partial, SEQ, 0, 0, tiled=True)
    back = exchange(back, -1)
    partial = after(partial, back)
    d_x = input_grads(idx, back, gate_full, w_in, x, grad_out[0], d_mid, w_score)
    last = lax.all_to_all(pack(partial), "dp", 0, 0, tiled=True)
    d_w_in, d_w_out, d_w_score, d_head = last_sum(last)
    return d_x[None], d_w_in, d_w_out, d_w_score, d_head.reshape(256)


def solution(mesh):
    inner = Mesh(mesh.devices.reshape(8, 4, 4, 2), ("dp", "x", "y", "core"))
    placed = (
        P("dp", SEQ, None),
        P("dp", None),
        P("dp", None),
        P(),
        P(),
        P(),
        P(),
        P("dp", SEQ, None),
        P("dp", SEQ),
    )
    return jax.shard_map(
        on_device,
        mesh=inner,
        in_specs=placed,
        out_specs=(P("dp", SEQ, None), P(SEQ, "dp"), P(SEQ, "dp"), P(SEQ, "dp"), P()),
        check_vma=False,
    )
```

```python
import functools

import jax
import jax.numpy as jnp
from jax import lax
from jax.experimental import pallas as pl
from jax.experimental.pallas import tpu as pltpu
from jax.sharding import Mesh
from jax.sharding import PartitionSpec as P

HEADS = 4
DH = 128
ROWS = 128
HIST = 8
TOKENS = 4096
DIVISOR = 2048.0
TILE = 256
PAIR = 4
NORM_EPS = 1e-05
SEQ = ("x", "y", "core")

f32 = jnp.float32
bf16 = jnp.bfloat16
VMEM = pl.BlockSpec(memory_space=pltpu.VMEM)
SMEM = pl.BlockSpec(memory_space=pltpu.SMEM)
HBM = pl.BlockSpec(memory_space=pltpu.HBM)
PARAMS = pltpu.CompilerParams(vmem_limit_bytes=16 * 1024 * 1024)


def cost(us):
    return pl.CostEstimate(flops=int(us * 1.15e9), bytes_accessed=0, transcendentals=0)


def shape(dims, kind):
    return jax.ShapeDtypeStruct(dims, kind)


def dot(a, b):
    return lax.dot_general(a, b, (((1,), (0,)), ((), ())), preferred_element_type=f32)


def dot_t(a, b):
    return lax.dot_general(a, b, (((1,), (1,)), ((), ())), preferred_element_type=f32)


def sigmoid(value):
    return 0.5 + 0.5 * jnp.tanh(0.5 * value)


def silu_slope(value):
    sigma = sigmoid(value)
    return sigma * (1.0 + value * (1.0 - sigma))


def norm_rows(value):
    centre = value - jnp.mean(value, axis=-1, keepdims=True)
    inverse = lax.rsqrt(jnp.mean(centre * centre, axis=-1, keepdims=True) + NORM_EPS)
    return centre * inverse, inverse


def norm_back(grad, normed, inverse):
    return inverse * (
        grad
        - jnp.mean(grad, axis=-1, keepdims=True)
        - normed * jnp.mean(grad * normed, axis=-1, keepdims=True)
    )


class Histories:
    def __init__(self, len_ref, tgt_ref):
        self.starts, self.ends, self.firsts = [], [], []
        total = jnp.int32(0)
        for h in range(HIST):
            length = len_ref[h]
            self.starts.append(total)
            total = total + length
            self.ends.append(total)
            self.firsts.append(total - jnp.minimum(tgt_ref[h], length - 1))

    def pick(self, values, pos):
        out = jnp.where(pos >= self.starts[1], values[1], values[0])
        for h in range(2, HIST):
            out = jnp.where(pos >= self.starts[h], values[h], out)
        return out

    def range_of(self, pos):
        return self.pick(self.starts, pos), jnp.minimum(self.pick(self.firsts, pos), pos + 1)


def copy_all(copies):
    for copy in copies:
        copy.start()
    return copies


def project_kernel(x_hbm, w_hbm, normed_ref, o0, o1, o2, o3, x_ref, w_ref, sems):
    width = HEADS * DH
    copies = copy_all(
        [pltpu.make_async_copy(x_hbm, x_ref, sems.at[3])]
        + [
            pltpu.make_async_copy(w_hbm.at[:, pl.ds(kind * width, width)], w_ref.at[i], sems.at[i])
            for i, kind in enumerate((3, 1, 2))
        ]
    )
    copies[0].wait()
    value, _ = norm_rows(x_ref[...].astype(f32))
    normed = value.astype(bf16)
    normed_ref[...] = normed
    for i in range(3):
        copies[i + 1].wait()
        pre = dot(normed, w_ref[i])
        hidden = (pre * sigmoid(pre)).astype(bf16)
        for h in range(HEADS):
            away = lax.rem(h - lax.axis_index("x") + HEADS, HEADS)
            for k, ref in enumerate((o0, o1, o2, o3)):

                @pl.when(away == k)
                def _(ref=ref, h=h):
                    ref[:, i * DH : (i + 1) * DH] = hidden[:, h * DH : (h + 1) * DH]


def project(x, w_in):
    out = pl.pallas_call(
        project_kernel,
        in_specs=[HBM, HBM],
        out_specs=[VMEM] * 5,
        out_shape=[shape((ROWS, 1024), bf16)] + [shape((ROWS, 3 * DH), bf16)] * 4,
        scratch_shapes=[
            pltpu.VMEM((ROWS, 1024), bf16),
            pltpu.VMEM((3, 1024, HEADS * DH), bf16),
            pltpu.SemaphoreType.DMA((4,)),
        ],
        compiler_params=pltpu.CompilerParams(vmem_limit_bytes=60 * 1024 * 1024),
        cost_estimate=cost(3),
        name="project",
    )(x, w_in)
    return out[0], out[1:5]


def gates_kernel(normed_ref, w_hbm, gate_ref, slope_ref, w_ref, sem):
    copy = pltpu.make_async_copy(w_hbm.at[:, pl.ds(0, HEADS * DH)], w_ref, sem)
    copy.start()
    copy.wait()
    pre = dot(normed_ref[...], w_ref[...])
    sigma = sigmoid(pre)
    gate_ref[...] = (pre * sigma).astype(bf16)
    slope_ref[...] = sigma * (1.0 + pre * (1.0 - sigma))


def gates(normed, w_in):
    width = HEADS * DH
    return pl.pallas_call(
        gates_kernel,
        in_specs=[VMEM, HBM],
        out_specs=[VMEM] * 2,
        out_shape=[shape((ROWS, width), bf16), shape((ROWS, width), f32)],
        scratch_shapes=[pltpu.VMEM((1024, width), bf16), pltpu.SemaphoreType.DMA],
        compiler_params=PARAMS,
        cost_estimate=cost(0.2),
        name="gates",
    )(normed, w_in)


def slopes_kernel(idx, n0, n1, n2, n3, w_hbm, out_ref, w_ref, sems):
    copies = []
    for i, kind in enumerate((2, 3, 1)):
        at = pl.ds(pl.multiple_of((kind * HEADS + idx[0]) * DH, DH), DH)
        copies.append(pltpu.make_async_copy(w_hbm.at[:, at], w_ref.at[i], sems.at[i]))
    copy_all(copies)
    for i in range(3):
        copies[i].wait()
        for k, ref in enumerate((n0, n1, n2, n3)):
            out_ref[k, :, i * DH : (i + 1) * DH] = silu_slope(dot(ref[...], w_ref[i]))


def slopes(idx, normed, w_in):
    return pl.pallas_call(
        slopes_kernel,
        in_specs=[SMEM] + [VMEM] * 4 + [HBM],
        out_specs=VMEM,
        out_shape=shape((4, ROWS, 3 * DH), f32),
        scratch_shapes=[pltpu.VMEM((3, 1024, DH), bf16), pltpu.SemaphoreType.DMA((3,))],
        compiler_params=PARAMS,
        cost_estimate=cost(0.5),
        name="slopes",
    )(idx, *normed, w_in)


def block_of(idx, k):
    return lax.rem(idx[0] - k + 4, 4) * 8 + idx[1] * 2 + idx[2]


WHOLE = [(j % 4, j // 4, 0, 4) for j in range(8)]
NEAR = [(0, 0, 0, 4), (1, 0, 0, 4), (3, 0, 0, 4), (0, 1, 0, 4), (1, 1, 0, 4), (3, 1, 0, 4)]


def assemble(idx, pieces, places, outs):
    for piece, (back, other, first, count) in zip(pieces, places, strict=True):
        at_y = lax.rem(idx[1] - back + 4, 4)
        at_core = 1 - idx[2] if other else idx[2]
        for i in range(count):
            block = lax.rem(idx[0] - first - i + 4, 4) * 8 + at_y * 2 + at_core
            where = pl.ds(pl.multiple_of(block * ROWS, ROWS), ROWS)
            for ref, column in outs:
                ref[where, :] = piece[i, :, column : column + DH]


def for_items(lows, highs, body):
    ends, total = [], jnp.int32(0)
    for low, high in zip(lows, highs, strict=True):
        total = total + (high - low + 1)
        ends.append(total)

    def step(i, carry):
        for j in range(PAIR):
            n = i * PAIR + j
            k, t = jnp.int32(0), n + lows[0]
            for q in range(1, 4):
                k = jnp.where(n >= ends[q - 1], q, k)
                t = jnp.where(n >= ends[q - 1], n - ends[q - 1] + lows[q], t)
            body(k, t, n < total)
        return carry

    lax.fori_loop(0, (total + PAIR - 1) // PAIR, step, 0)


def tile_at(t):
    return pl.ds(pl.multiple_of(jnp.minimum(t, TOKENS // TILE - 1) * TILE, TILE), TILE)


def set_marks(idx, hist, marks):
    row = lax.broadcasted_iota(jnp.int32, (ROWS, 128), 0)
    lows, highs = [], []
    for k in range(4):
        first = block_of(idx, k) * ROWS
        start, limit = hist.range_of(first + row)
        marks[0, k], marks[1, k] = start, limit
        lows.append(hist.pick(hist.starts, first) // TILE)
        highs.append(first // TILE)
    return lows, highs


def seen_by(idx, marks, k, t):
    row = lax.broadcasted_iota(jnp.int32, (ROWS, TILE), 0)
    lane = lax.broadcasted_iota(jnp.int32, (ROWS, TILE), 1)
    key = lane + t * TILE
    start, limit = [jnp.concatenate([marks[i, k]] * (TILE // 128), axis=1) for i in range(2)]
    return ((key >= start) & (key < limit)) | (key - row == block_of(idx, k) * ROWS)


def attend(idx, marks, q_own, total, k, t, keys, values):
    half = dot_t(q_own[k], keys) * (0.5 * DH**-0.5)
    weight = half * (1.0 + jnp.tanh(half))
    weight = jnp.where(seen_by(idx, marks, k, t), weight, 0.0).astype(bf16)
    total[k] += dot(weight, values)


def near_kernel(idx, len_ref, tgt_ref, *refs):
    pieces, out, all_hbm = refs[0:6], refs[6], refs[7:10]
    k_all, v_all, q_all, q_own, marks, sems = refs[10:16]
    hist = Histories(len_ref, tgt_ref)
    for x in range(4):
        at = pl.ds(pl.multiple_of((x * 4 + lax.rem(idx[1] + 2, 4)) * TILE, TILE), TILE)
        for ref in (k_all, v_all, q_all):
            ref[at, :] = jnp.zeros((TILE, DH), bf16)
    assemble(idx, pieces, NEAR, [(k_all, 0), (v_all, DH), (q_all, 2 * DH)])
    copies = copy_all(
        [
            pltpu.make_async_copy(ref, all_hbm[i], sems.at[i])
            for i, ref in enumerate((k_all, v_all, q_all))
        ]
    )
    for k in range(4):
        q_own[k] = pieces[0][k, :, 2 * DH : 3 * DH]
    out[...] = jnp.zeros_like(out)
    lows, highs = set_marks(idx, hist, marks)
    base = 3 - lax.rem(idx[1] + 2, 4)
    lows = [(low + base) // 4 * 3 + jnp.minimum((low + base) % 4, 3) for low in lows]
    highs = [(high + base) // 4 * 3 + jnp.minimum((high + base) % 4, 2) for high in highs]

    def body(k, u, valid):
        t = u + u // 3 - base
        at = tile_at(t)
        attend(idx, marks, q_own, out, k, t, k_all[at, :], v_all[at, :])

    for_items(lows, highs, body)
    for copy in copies:
        copy.wait()


def attend_near(idx, lengths, targets, pieces):
    return pl.pallas_call(
        near_kernel,
        in_specs=[SMEM] * 3 + [VMEM] * 6,
        out_specs=[VMEM] + [HBM] * 3,
        out_shape=[shape((4, ROWS, DH), f32)] + [shape((TOKENS, DH), bf16)] * 3,
        scratch_shapes=[pltpu.VMEM((TOKENS, DH), bf16)] * 3
        + [
            pltpu.VMEM((4, ROWS, DH), bf16),
            pltpu.VMEM((2, 4, ROWS, 128), jnp.int32),
            pltpu.SemaphoreType.DMA((3,)),
        ],
        compiler_params=PARAMS,
        cost_estimate=cost(0.5),
        name="attend_near",
    )(idx, lengths, targets, *pieces)


def far_kernel(idx, len_ref, tgt_ref, *refs):
    held, pieces, near, o_refs, all_hbm = refs[0], refs[1:5], refs[5], refs[9:13], refs[13:16]
    k_far, v_far, q_far, q_own, total, marks, sems = refs[16:23]
    hist = Histories(len_ref, tgt_ref)
    far = lax.rem(idx[1] + 2, 4)
    for j in range(4):
        other, first = j // 2, j % 2 * 2
        at_core = 1 - idx[2] if other else idx[2]
        for i in range(2):
            x = lax.rem(idx[0] - first - i + 4, 4)
            where = pl.ds(pl.multiple_of(x * TILE + at_core * ROWS, ROWS), ROWS)
            for n, ref in enumerate((k_far, v_far, q_far)):
                ref[where, :] = pieces[j][i, :, n * DH : (n + 1) * DH]
    copies = []
    for x in range(4):
        at = pl.ds(pl.multiple_of((x * 4 + far) * TILE, TILE), TILE)
        for n, ref in enumerate((k_far, v_far, q_far)):
            tile = ref.at[x * TILE : (x + 1) * TILE, :]
            copies.append(pltpu.make_async_copy(tile, all_hbm[n].at[at, :], sems.at[x * 3 + n]))
    copy_all(copies)
    for k in range(4):
        q_own[k] = held[k, :, 2 * DH : 3 * DH]
    total[...] = near[...]
    lows, highs = set_marks(idx, hist, marks)
    lows = [(low - far + 3) // 4 for low in lows]
    highs = [(high - far + 4) // 4 - 1 for high in highs]

    def body(k, u, valid):
        at = pl.ds(pl.multiple_of(jnp.minimum(u, 3) * TILE, TILE), TILE)
        attend(idx, marks, q_own, total, k, u * 4 + far, k_far[at, :], v_far[at, :])

    for_items(lows, highs, body)
    for k in range(4):
        o_refs[k][...] = total[k] * (1.0 / DIVISOR)
    for copy in copies:
        copy.wait()


def attend_far(idx, lengths, targets, held, pieces, near, everything):
    return pl.pallas_call(
        far_kernel,
        in_specs=[SMEM] * 3 + [VMEM] * 6 + [HBM] * 3,
        out_specs=[VMEM] * 4 + [HBM] * 3,
        out_shape=[shape((ROWS, DH), f32)] * 4 + [shape((TOKENS, DH), bf16)] * 3,
        input_output_aliases={9: 4, 10: 5, 11: 6},
        scratch_shapes=[pltpu.VMEM((4 * TILE, DH), bf16)] * 3
        + [
            pltpu.VMEM((4, ROWS, DH), bf16),
            pltpu.VMEM((4, ROWS, DH), f32),
            pltpu.VMEM((2, 4, ROWS, 128), jnp.int32),
            pltpu.SemaphoreType.DMA((12,)),
        ],
        compiler_params=PARAMS,
        cost_estimate=cost(0.5),
        name="attend_far",
    )(idx, lengths, targets, held, *pieces, near, *everything)


def two_of(head):
    high = head.astype(bf16).astype(f32)
    return high, (head - high).astype(bf16).astype(f32)


def with_head(rows, head, count):
    high, low = two_of(head)
    width = ACTS if rows is None else rows.shape[1]
    line = jnp.concatenate([high, low, jnp.zeros((1, width - 512), f32)], axis=1)
    line = jnp.concatenate([line, jnp.zeros((count - 1, width), f32)], axis=0)
    return (line if rows is None else jnp.concatenate([rows, line], axis=0)).astype(bf16)


def head_of(value, row):
    return value[row : row + 1, 0:256] + value[row : row + 1, 256:512]


ACTS = 512 + 1024 + 1024 + 256


def middle_kernel(idx, len_ref, tgt_ref, a0, a1, a2, a3, gate_ref, slope_ref, x_ref, w_out, w_score, head, grad, score, *refs):
    d_refs, g_full, acts, mid_ref = refs[0:4], refs[4], refs[5], refs[6]
    att, work = refs[7:9]
    for k, ref in enumerate((a0, a1, a2, a3)):
        at = pl.ds(pl.multiple_of(lax.rem(idx[0] + k, 4) * DH, DH), DH)
        att[:, at] = ref[...]
    onorm, inverse = norm_rows(att[...])
    gate = gate_ref[...].astype(f32)
    gated = (onorm * gate).astype(bf16)
    acts[0:ROWS, 0:512] = gated
    out_b = (x_ref[...].astype(f32) + dot(gated, w_out[...])).astype(bf16)
    acts[0:ROWS, 1536:2560] = out_b
    mid = dot(out_b, w_score[...])
    hist = Histories(len_ref, tgt_ref)
    own = ((idx[0] * 4 + idx[1]) * 2 + idx[2]) * ROWS
    pos = own + lax.broadcasted_iota(jnp.int32, (ROWS, 1), 0)
    diagonal = lax.broadcasted_iota(jnp.int32, (ROWS, ROWS), 0) == lax.broadcasted_iota(
        jnp.int32, (ROWS, ROWS), 1
    )
    column = jnp.sum(jnp.where(diagonal, score[...], 0.0), axis=1, keepdims=True)
    weight = jnp.where(pos >= hist.pick(hist.firsts, pos), column, 0.0)
    sigma = sigmoid(mid)
    head_part = jnp.sum(weight * (mid * sigma), axis=0, keepdims=True)
    acts[ROWS : ROWS + 16, :] = with_head(None, head_part, 16)
    d_mid = (weight * head[...] * (sigma * (1.0 + mid * (1.0 - sigma)))).astype(bf16)
    acts[0:ROWS, 2560:2816] = d_mid
    mid_ref[...] = d_mid
    total_b = (grad[...].astype(f32) + dot_t(d_mid, w_score[...])).astype(bf16)
    acts[0:ROWS, 512:1536] = total_b
    d_gated = dot_t(total_b, w_out[...])
    att[...] = norm_back(d_gated * gate, onorm, inverse)
    work[...] = d_gated * onorm * slope_ref[...]
    g_full[...] = work[...].astype(bf16)
    for k in range(4):
        at = pl.ds(pl.multiple_of(lax.rem(idx[0] + k, 4) * DH, DH), DH)
        d_refs[k][:, 0:DH] = att[:, at].astype(bf16)
        d_refs[k][:, DH : 2 * DH] = work[:, at].astype(bf16)


def middle(idx, lengths, targets, attended, gate, slope, x, w_out, w_score, head, grad, score):
    width = HEADS * DH
    return pl.pallas_call(
        middle_kernel,
        in_specs=[SMEM] * 3 + [VMEM] * 12,
        out_specs=[VMEM] * 7,
        out_shape=[shape((ROWS, 2 * DH), bf16)] * 4
        + [
            shape((ROWS, width), bf16),
            shape((ROWS + 16, ACTS), bf16),
            shape((ROWS, 256), bf16),
        ],
        scratch_shapes=[pltpu.VMEM((ROWS, width), f32)] * 2,
        compiler_params=PARAMS,
        cost_estimate=cost(0.5),
        name="middle",
    )(idx, lengths, targets, *attended, gate, slope, x, w_out, w_score, head, grad, score)


SLOPE_SCALE = 0.5 * 2**-0.5
SLOPE_REST = DH**-0.5 / DIVISOR / 2**-0.5


def query_kernel(idx, len_ref, tgt_ref, *refs):
    held, d_refs, (k_all, v_all), out_refs = refs[0], refs[1:5], refs[5:7], refs[7:11]
    q_own, d_own, total, marks = refs[11:15]
    hist = Histories(len_ref, tgt_ref)
    for k in range(4):
        q_own[k] = held[k, :, 2 * DH : 3 * DH]
        d_own[k] = d_refs[k][:, 0:DH]
    total[...] = jnp.zeros_like(total)
    lows, highs = set_marks(idx, hist, marks)

    def body(k, t, valid):
        at = tile_at(t)
        keys = k_all[at, :]
        half = dot_t(q_own[k], keys) * (0.5 * DH**-0.5)
        d_attn = dot_t(d_own[k], v_all[at, :])
        tanh = jnp.tanh(half)
        factor = (SLOPE_SCALE + SLOPE_SCALE * tanh) * (1.0 + half * (1.0 - tanh))
        d_raw = jnp.where(seen_by(idx, marks, k, t), d_attn * factor, 0.0).astype(bf16)
        total[k] += dot(d_raw, keys)

    for_items(lows, highs, body)
    for k in range(4):
        out_refs[k][...] = total[k] * SLOPE_REST


def query_grads(idx, lengths, targets, held, d_att, k_all, v_all):
    return pl.pallas_call(
        query_kernel,
        in_specs=[SMEM] * 3 + [VMEM] * 7,
        out_specs=[VMEM] * 4,
        out_shape=[shape((ROWS, DH), f32)] * 4,
        scratch_shapes=[pltpu.VMEM((4, ROWS, DH), bf16)] * 2
        + [pltpu.VMEM((4, ROWS, DH), f32), pltpu.VMEM((2, 4, ROWS, 128), jnp.int32)],
        compiler_params=PARAMS,
        cost_estimate=cost(3),
        name="query_grads",
    )(idx, lengths, targets, held, *d_att, k_all, v_all)


def key_kernel(idx, len_ref, tgt_ref, *refs):
    d_pieces, (k_hbm, v_hbm, q_hbm, slope_ref) = refs[0:8], refs[8:12]
    dq_refs, d_refs, back_refs, all_ref = refs[12:16], refs[16:20], refs[20:24], refs[24]
    q_all, d_all, k_own, v_own, d_key, d_value, sems = refs[25:32]
    copies = [pltpu.make_async_copy(q_hbm, q_all, sems.at[8])]
    for k in range(4):
        at = pl.ds(pl.multiple_of(block_of(idx, k) * ROWS, ROWS), ROWS)
        copies.append(pltpu.make_async_copy(k_hbm.at[at, :], k_own.at[k], sems.at[k]))
        copies.append(pltpu.make_async_copy(v_hbm.at[at, :], v_own.at[k], sems.at[k + 4]))
    copy_all(copies)
    hist = Histories(len_ref, tgt_ref)
    assemble(idx, d_pieces, WHOLE, [(d_all, 0)])
    d_key[...] = jnp.zeros_like(d_key)
    d_value[...] = jnp.zeros_like(d_value)
    row = lax.broadcasted_iota(jnp.int32, (ROWS, TILE), 0)
    lane = lax.broadcasted_iota(jnp.int32, (1, TILE), 1)
    lows, highs = [], []
    for k in range(4):
        first = block_of(idx, k) * ROWS
        lows.append(first // TILE)
        highs.append((hist.pick(hist.ends, first + ROWS - 1) - 1) // TILE)
    for copy in copies:
        copy.wait()

    def body(k, t, valid):
        at = tile_at(t)
        queries, d_att = q_all[at, :], d_all[at, :]
        half = dot_t(k_own[k], queries) * (0.5 * DH**-0.5)
        d_attn = dot_t(v_own[k], d_att)
        key = block_of(idx, k) * ROWS + row
        pos = lane + t * TILE
        start, limit = hist.range_of(pos)
        start = start + jnp.where(valid, 0, TOKENS)
        seen = ((key >= start) & (key < limit)) | (key == pos)
        tanh = jnp.tanh(half)
        more = 1.0 + tanh
        weight = jnp.where(seen, half * more, 0.0).astype(bf16)
        factor = (SLOPE_SCALE * more) * (1.0 + half * (1.0 - tanh))
        d_raw = jnp.where(seen, d_attn * factor, 0.0).astype(bf16)
        d_key[k] += dot(d_raw, queries)
        d_value[k] += dot(weight, d_att)

    for_items(lows, highs, body)
    for k in range(4):
        d_q = (dq_refs[k][...] * slope_ref[k, :, 0:DH]).astype(bf16)
        d_k = (d_key[k] * SLOPE_REST * slope_ref[k, :, DH : 2 * DH]).astype(bf16)
        d_v = (d_value[k] * (1.0 / DIVISOR) * slope_ref[k, :, 2 * DH : 3 * DH]).astype(bf16)
        back_refs[k][:, 0:DH] = d_v
        back_refs[k][:, DH : 2 * DH] = d_q
        back_refs[k][:, 2 * DH : 3 * DH] = d_k
        at = pl.ds(k * ROWS, ROWS)
        all_ref[at, 0:DH] = d_refs[k][:, DH : 2 * DH]
        all_ref[at, DH : 2 * DH] = d_v
        all_ref[at, 2 * DH : 3 * DH] = d_q
        all_ref[at, 3 * DH : 4 * DH] = d_k


def key_grads(idx, lengths, targets, d_pieces, everything, slope, d_query, d_att):
    return pl.pallas_call(
        key_kernel,
        in_specs=[SMEM] * 3 + [VMEM] * 8 + [HBM] * 3 + [VMEM] * 9,
        out_specs=[VMEM] * 5,
        out_shape=[shape((ROWS, 3 * DH), bf16)] * 4 + [shape((4 * ROWS, 4 * DH), bf16)],
        scratch_shapes=[pltpu.VMEM((TOKENS, DH), bf16)] * 2
        + [pltpu.VMEM((4, ROWS, DH), bf16)] * 2
        + [pltpu.VMEM((4, ROWS, DH), f32)] * 2
        + [pltpu.SemaphoreType.DMA((9,))],
        compiler_params=PARAMS,
        cost_estimate=cost(0.02),
        name="key_grads",
    )(idx, lengths, targets, *d_pieces, *everything, slope, *d_query, *d_att)


def dot_first(a, b):
    return lax.dot_general(a, b, (((0,), (0,)), ((), ())), preferred_element_type=f32)


def parts_kernel(idx, own, got, out, rows):
    rows[0:ROWS, :] = own[0:ROWS, :]
    rows[ROWS : 2 * ROWS, :] = got[0:ROWS, :]
    total = rows[:, pl.ds(pl.multiple_of(512 + idx[2] * 512, 512), 512)]
    d_mid = rows[:, pl.ds(pl.multiple_of(2560 + idx[2] * 128, 128), 128)]
    head = [head_of(ref[ROWS : ROWS + 16, 0:512].astype(f32), 0) for ref in (own, got)]
    high, low = two_of(head[0] + head[1])
    line = jnp.concatenate([high, low], axis=1)
    line = jnp.concatenate([line, jnp.zeros((7, 512), f32)], axis=0)
    for x in range(4):
        part = dot_first(rows[:, x * 128 : (x + 1) * 128], total)
        score = dot_first(rows[:, 1536 + x * 256 : 1792 + x * 256], d_mid)
        for m in range(8):
            last = [score[m * 32 + j * 8 : m * 32 + (j + 1) * 8] for j in range(4)]
            block = [part[m * 16 : (m + 1) * 16], jnp.concatenate(last, axis=1), line]
            out[x * 8 + m] = jnp.concatenate(block, axis=0).astype(bf16)


def parts(idx, own, got):
    return pl.pallas_call(
        parts_kernel,
        in_specs=[SMEM] + [VMEM] * 2,
        out_specs=VMEM,
        out_shape=shape((32, 32, 512), bf16),
        scratch_shapes=[pltpu.VMEM((2 * ROWS, ACTS), bf16)],
        compiler_params=PARAMS,
        cost_estimate=cost(0.3),
        name="parts",
    )(idx, own, got)


def weights_kernel(away, idx, n0, n1, n2, n3, d_pre, out, left):
    for k, ref in enumerate((n0, n1, n2, n3)):
        left[k * ROWS : (k + 1) * ROWS, :] = ref[...]
    half = idx[2] if away == 0 else 1 - idx[2]
    right = d_pre[:, pl.ds(pl.multiple_of(half * 256, 256), 256)]
    for n in range(4):
        part = dot_first(left[:, n * 256 : (n + 1) * 256], right)
        for i in range(8):
            rows = [part[i * 32 : i * 32 + 16], part[i * 32 + 16 : (i + 1) * 32]]
            out[n * 8 + i] = jnp.concatenate(rows, axis=1).astype(out.dtype)


def weights(away, idx, normed, d_pre):
    return pl.pallas_call(
        functools.partial(weights_kernel, away),
        in_specs=[SMEM] + [VMEM] * 5,
        out_specs=VMEM,
        out_shape=shape((32, 16, 512), bf16 if away else f32),
        scratch_shapes=[pltpu.VMEM((512, 1024), bf16)],
        compiler_params=PARAMS,
        cost_estimate=cost(0.02),
        name="weights",
    )(idx, *normed, d_pre)


def merge_kernel(keep, got, early, out):
    for n in range(32):
        out[n, 0:16, :] = (keep[n] + got[n].astype(f32)).astype(bf16)
        out[n, 16:48, :] = early[n]


def merge(keep, got, early):
    return pl.pallas_call(
        merge_kernel,
        in_specs=[VMEM] * 3,
        out_specs=VMEM,
        out_shape=shape((32, 48, 512), bf16),
        compiler_params=PARAMS,
        cost_estimate=cost(0.3),
        name="merge",
    )(keep, got, early)


def pack_kernel(ref, out_ref):
    for c in range(2):
        for h in range(HEADS):
            total = ref[h * 8 + c, 0:16, :].astype(f32)
            for n in range(1, 4):
                total = total + ref[h * 8 + n * 2 + c, 0:16, :].astype(f32)
            for i in range(2):
                z, half = divmod((c * 2 + i) * HEADS + h, 2)
                rows = [total[:, r * 256 + i * 128 : r * 256 + (i + 1) * 128] for r in range(2)]
                rows = jnp.concatenate(rows, axis=0).astype(bf16)
                out_ref[z, half * 32 : (half + 1) * 32, :] = rows
    sums = []
    for c in range(2):
        total = ref[c, 16:48, :].astype(f32)
        head = head_of(total, 24)
        for n in range(c + 2, 32, 2):
            part = ref[n, 16:48, :].astype(f32)
            total, head = total + part, head + head_of(part, 24)
        sums.append(total)
    high, low = two_of(head)
    head = [high[:, 0:128], high[:, 128:256], low[:, 0:128], low[:, 128:256]]
    head = jnp.concatenate(head + [jnp.zeros((4, 128), f32)], axis=0)
    for z in range(8):
        total, at = sums[z // 4], z % 4 * 128
        score = [total[16:24, j * 128 + z % 4 * 32 : j * 128 + z % 4 * 32 + 32] for j in range(4)]
        rows = [total[0:16, at : at + 128], jnp.concatenate(score, axis=1), head]
        out_ref[z, 64:96, :] = jnp.concatenate(rows, axis=0).astype(bf16)


def pack(value):
    return pl.pallas_call(
        pack_kernel,
        in_specs=[VMEM],
        out_specs=VMEM,
        out_shape=shape((8, 96, 128), bf16),
        compiler_params=PARAMS,
        cost_estimate=cost(2),
        name="pack",
    )(value)


def last_kernel(ref, in_ref, out_ref, score_ref, head_ref):
    total = ref[0].astype(f32)
    for z in range(1, 8):
        total = total + ref[z].astype(f32)
    in_ref[:, 0:128] = total[0:32]
    in_ref[:, 128:256] = total[32:64]
    out_ref[...] = total[64:80]
    for j in range(4):
        score_ref[j * 8 : (j + 1) * 8, :] = total[80:88, j * 32 : (j + 1) * 32]
    head_ref[:, 0:128] = total[88:89] + total[90:91]
    head_ref[:, 128:256] = total[89:90] + total[91:92]


def last_sum(value):
    return pl.pallas_call(
        last_kernel,
        in_specs=[VMEM],
        out_specs=[VMEM] * 4,
        out_shape=[
            shape((32, 256), f32),
            shape((16, 128), f32),
            shape((32, 32), f32),
            shape((1, 256), f32),
        ],
        compiler_params=PARAMS,
        cost_estimate=cost(1),
        name="last_sum",
    )(value)


def input_kernel(idx, b0, b1, b2, b3, gate_ref, w_ref, x_ref, grad, d_mid, w_score, out_ref, d_pre, d_norm):
    step = pl.program_id(0)
    width = HEADS * DH

    @pl.when(step == 0)
    def _():
        d_pre[:, 0:width] = gate_ref[...]
        for k, ref in enumerate((b0, b1, b2, b3)):
            head = lax.rem(idx[0] + k, 4)
            for kind in range(3):
                at = pl.ds(pl.multiple_of((kind + 1) * width + head * DH, DH), DH)
                d_pre[:, at] = ref[:, kind * DH : (kind + 1) * DH]

    d_norm[:, pl.ds(pl.multiple_of(step * 256, 256), 256)] = dot_t(d_pre[...], w_ref[...])

    @pl.when(step == 3)
    def _():
        normed, inverse = norm_rows(x_ref[...].astype(f32))
        d_total = grad[...].astype(f32) + dot_t(d_mid[...], w_score[...])
        out_ref[...] = (d_total + norm_back(d_norm[...], normed, inverse)).astype(bf16)


def input_grads(idx, back, gate, w_in, x, grad, d_mid, w_score):
    whole = lambda dims: pl.BlockSpec(dims, lambda i: (0, 0))
    return pl.pallas_call(
        input_kernel,
        grid=(4,),
        in_specs=[SMEM]
        + [whole((ROWS, 3 * DH))] * 4
        + [
            whole((ROWS, HEADS * DH)),
            pl.BlockSpec((256, 2048), lambda i: (i, 0)),
            whole((ROWS, 1024)),
            whole((ROWS, 1024)),
            whole((ROWS, 256)),
            whole((1024, 256)),
        ],
        out_specs=whole((ROWS, 1024)),
        out_shape=shape((ROWS, 1024), bf16),
        scratch_shapes=[pltpu.VMEM((ROWS, 2048), bf16), pltpu.VMEM((ROWS, 1024), f32)],
        compiler_params=PARAMS,
        cost_estimate=cost(4),
        name="input_grads",
    )(idx, *back, gate, w_in, x, grad, d_mid, w_score)


def join_kernel(*refs):
    for k in range(4):
        refs[4][k] = refs[k][:, 0 : refs[4].shape[2]]


def join(arrays, width):
    return pl.pallas_call(
        join_kernel,
        in_specs=[VMEM] * 4,
        out_specs=VMEM,
        out_shape=shape((4, ROWS, width), bf16),
        compiler_params=PARAMS,
        cost_estimate=cost(0.1),
        name="join",
    )(*arrays)


def halves_kernel(back, ahead, low, high):
    low[...] = back[0:2]
    high[...] = ahead[2:4]


def halves(back, ahead):
    return pl.pallas_call(
        halves_kernel,
        in_specs=[VMEM] * 2,
        out_specs=[VMEM] * 2,
        out_shape=[shape((2,) + back.shape[1:], bf16)] * 2,
        compiler_params=PARAMS,
        cost_estimate=cost(0.1),
        name="halves",
    )(back, ahead)


def shifted(value, axis, by):
    size = lax.axis_size(axis)
    return lax.ppermute(value, axis, [(i, (i + by) % size) for i in range(size)])


def swapped(value, axis, bit):
    return lax.ppermute(value, axis, [(i, i ^ bit) for i in range(lax.axis_size(axis))])


def after(value, other):
    return lax.optimization_barrier((value, other))[0]


def exchange(values, sign):
    return [values[0]] + [shifted(values[k], "x", sign * k) for k in range(1, 4)]


def with_core(pieces):
    return pieces + [swapped(piece, "core", 1) for piece in pieces]


def gathered_ring(value):
    near = [value, shifted(value, "y", 1), shifted(value, "y", -1)]
    low, high = halves(near[1], near[2])
    far = [shifted(low, "y", 1), shifted(high, "y", -1)]
    return with_core(near), far


def on_device(x_rows, lengths, targets, w_in, w_out, w_score, head_score, grad_out, grad_score):
    x, lengths, targets = x_rows[0], lengths[0], targets[0]
    idx = jnp.stack([lax.axis_index(a) for a in SEQ]).astype(jnp.int32)
    normed, kvq = project(x, w_in)
    kvq = exchange(kvq, 1)
    held = join(kvq, 3 * DH)
    near_pieces, far_pieces = gathered_ring(held)
    normed = after(normed, kvq[3])
    near = [shifted(normed, "x", 1), shifted(normed, "x", -1)]
    normed_all = [normed, near[0], shifted(after(normed, near), "x", 2), near[1]]
    partly = attend_near(idx, lengths, targets, near_pieces)
    far_pieces, near, partly = lax.optimization_barrier((far_pieces, near, partly))
    far_pieces = with_core(far_pieces)
    forwarded = attend_far(idx, lengths, targets, held, far_pieces, partly[0], partly[1:4])
    k_all, v_all, q_all = forwarded[4:7]
    attended = exchange(forwarded[0:4], -1)
    gate, gate_slope = gates(after(normed, forwarded[0]), w_in)
    slope = slopes(idx, after(normed_all, forwarded[0]), w_in)
    attended = after(attended, slope)
    mid = middle(
        idx, lengths, targets, attended, gate, gate_slope, x, w_out, w_score,
        head_score.reshape(1, 256), grad_out[0], grad_score,
    )
    gate_full, acts, d_mid = mid[4:7]
    d_att = exchange(mid[0:4], 1)
    acts_other = swapped(after(acts, d_att), "core", 1)
    d_own = join(d_att, DH)
    late = [shifted(d_own, "y", k) for k in range(1, 4)]
    d_query = query_grads(idx, lengths, targets, held, d_att, k_all, v_all)
    d_pieces = with_core([d_own] + after(late, d_query[0]))
    keyed = key_grads(
        idx, lengths, targets, d_pieces, (k_all, v_all, q_all), slope, d_query, d_att
    )
    send = weights(1, idx, normed_all, keyed[4])
    got = swapped(send, "core", 1)
    keep = weights(0, idx, normed_all, after(keyed[4], send))
    early = parts(idx, after(acts, send), acts_other)
    partial = merge(keep, got, early)
    back, partial = lax.optimization_barrier((keyed[0:4], partial))
    partial = lax.all_to_all(partial, SEQ, 0, 0, tiled=True)
    back = exchange(back, -1)
    d_x = input_grads(idx, back, gate_full, w_in, x, grad_out[0], d_mid, w_score)
    last = lax.all_to_all(pack(partial), "dp", 0, 0, tiled=True)
    d_w_in, d_w_out, d_w_score, d_head = last_sum(last)
    return d_x[None], d_w_in, d_w_out, d_w_score, d_head.reshape(256)


def solution(mesh):
    inner = Mesh(mesh.devices.reshape(8, 4, 4, 2), ("dp", "x", "y", "core"))
    placed = (
        P("dp", SEQ, None),
        P("dp", None),
        P("dp", None),
        P(),
        P(),
        P(),
        P(),
        P("dp", SEQ, None),
        P("dp", SEQ),
    )
    return jax.shard_map(
        on_device,
        mesh=inner,
        in_specs=placed,
        out_specs=(P("dp", SEQ, None), P(SEQ, "dp"), P(SEQ, "dp"), P(SEQ, "dp"), P()),
        check_vma=False,
    )
```

```python
import functools

import jax
import jax.numpy as jnp
from jax import lax
from jax.experimental import pallas as pl
from jax.experimental.pallas import tpu as pltpu
from jax.sharding import Mesh
from jax.sharding import PartitionSpec as P

HEADS = 4
DH = 128
ROWS = 128
HIST = 8
TOKENS = 4096
DIVISOR = 2048.0
TILE = 256
PAIR = 4
NORM_EPS = 1e-05
SEQ = ("x", "y", "core")

f32 = jnp.float32
bf16 = jnp.bfloat16
VMEM = pl.BlockSpec(memory_space=pltpu.VMEM)
SMEM = pl.BlockSpec(memory_space=pltpu.SMEM)
HBM = pl.BlockSpec(memory_space=pltpu.HBM)
PARAMS = pltpu.CompilerParams(vmem_limit_bytes=16 * 1024 * 1024)


def cost(us):
    return pl.CostEstimate(flops=int(us * 1.15e9), bytes_accessed=0, transcendentals=0)


def shape(dims, kind):
    return jax.ShapeDtypeStruct(dims, kind)


def dot(a, b):
    return lax.dot_general(a, b, (((1,), (0,)), ((), ())), preferred_element_type=f32)


def dot_t(a, b):
    return lax.dot_general(a, b, (((1,), (1,)), ((), ())), preferred_element_type=f32)


def sigmoid(value):
    return 0.5 + 0.5 * jnp.tanh(0.5 * value)


def silu_slope(value):
    sigma = sigmoid(value)
    return sigma * (1.0 + value * (1.0 - sigma))


def norm_rows(value):
    centre = value - jnp.mean(value, axis=-1, keepdims=True)
    inverse = lax.rsqrt(jnp.mean(centre * centre, axis=-1, keepdims=True) + NORM_EPS)
    return centre * inverse, inverse


def norm_back(grad, normed, inverse):
    return inverse * (
        grad
        - jnp.mean(grad, axis=-1, keepdims=True)
        - normed * jnp.mean(grad * normed, axis=-1, keepdims=True)
    )


class Histories:
    def __init__(self, len_ref, tgt_ref):
        self.starts, self.ends, self.firsts = [], [], []
        total = jnp.int32(0)
        for h in range(HIST):
            length = len_ref[h]
            self.starts.append(total)
            total = total + length
            self.ends.append(total)
            self.firsts.append(total - jnp.minimum(tgt_ref[h], length - 1))

    def pick(self, values, pos):
        out = jnp.where(pos >= self.starts[1], values[1], values[0])
        for h in range(2, HIST):
            out = jnp.where(pos >= self.starts[h], values[h], out)
        return out

    def range_of(self, pos):
        return self.pick(self.starts, pos), jnp.minimum(self.pick(self.firsts, pos), pos + 1)


def copy_all(copies):
    for copy in copies:
        copy.start()
    return copies


def project_kernel(x_hbm, w_hbm, normed_ref, o0, o1, o2, o3, x_ref, w_ref, sems):
    width = HEADS * DH
    copies = copy_all(
        [pltpu.make_async_copy(x_hbm, x_ref, sems.at[3])]
        + [
            pltpu.make_async_copy(w_hbm.at[:, pl.ds(kind * width, width)], w_ref.at[i], sems.at[i])
            for i, kind in enumerate((3, 1, 2))
        ]
    )
    copies[0].wait()
    value, _ = norm_rows(x_ref[...].astype(f32))
    normed = value.astype(bf16)
    normed_ref[...] = normed
    for i in range(3):
        copies[i + 1].wait()
        pre = dot(normed, w_ref[i])
        hidden = (pre * sigmoid(pre)).astype(bf16)
        for h in range(HEADS):
            away = lax.rem(h - lax.axis_index("x") + HEADS, HEADS)
            for k, ref in enumerate((o0, o1, o2, o3)):

                @pl.when(away == k)
                def _(ref=ref, h=h):
                    ref[:, i * DH : (i + 1) * DH] = hidden[:, h * DH : (h + 1) * DH]


def project(x, w_in):
    out = pl.pallas_call(
        project_kernel,
        in_specs=[HBM, HBM],
        out_specs=[VMEM] * 5,
        out_shape=[shape((ROWS, 1024), bf16)] + [shape((ROWS, 3 * DH), bf16)] * 4,
        scratch_shapes=[
            pltpu.VMEM((ROWS, 1024), bf16),
            pltpu.VMEM((3, 1024, HEADS * DH), bf16),
            pltpu.SemaphoreType.DMA((4,)),
        ],
        compiler_params=pltpu.CompilerParams(vmem_limit_bytes=60 * 1024 * 1024),
        cost_estimate=cost(3),
        name="project",
    )(x, w_in)
    return out[0], out[1:5]


def gates_kernel(normed_ref, w_hbm, gate_ref, slope_ref, w_ref, sem):
    copy = pltpu.make_async_copy(w_hbm.at[:, pl.ds(0, HEADS * DH)], w_ref, sem)
    copy.start()
    copy.wait()
    pre = dot(normed_ref[...], w_ref[...])
    sigma = sigmoid(pre)
    gate_ref[...] = (pre * sigma).astype(bf16)
    slope_ref[...] = sigma * (1.0 + pre * (1.0 - sigma))


def gates(normed, w_in):
    width = HEADS * DH
    return pl.pallas_call(
        gates_kernel,
        in_specs=[VMEM, HBM],
        out_specs=[VMEM] * 2,
        out_shape=[shape((ROWS, width), bf16), shape((ROWS, width), f32)],
        scratch_shapes=[pltpu.VMEM((1024, width), bf16), pltpu.SemaphoreType.DMA],
        compiler_params=PARAMS,
        cost_estimate=cost(0.2),
        name="gates",
    )(normed, w_in)


def slopes_kernel(idx, n0, n1, n2, n3, w_hbm, out_ref, w_ref, sems):
    copies = []
    for i, kind in enumerate((2, 3, 1)):
        at = pl.ds(pl.multiple_of((kind * HEADS + idx[0]) * DH, DH), DH)
        copies.append(pltpu.make_async_copy(w_hbm.at[:, at], w_ref.at[i], sems.at[i]))
    copy_all(copies)
    for i in range(3):
        copies[i].wait()
        for k, ref in enumerate((n0, n1, n2, n3)):
            out_ref[k, :, i * DH : (i + 1) * DH] = silu_slope(dot(ref[...], w_ref[i]))


def slopes(idx, normed, w_in):
    return pl.pallas_call(
        slopes_kernel,
        in_specs=[SMEM] + [VMEM] * 4 + [HBM],
        out_specs=VMEM,
        out_shape=shape((4, ROWS, 3 * DH), f32),
        scratch_shapes=[pltpu.VMEM((3, 1024, DH), bf16), pltpu.SemaphoreType.DMA((3,))],
        compiler_params=PARAMS,
        cost_estimate=cost(0.5),
        name="slopes",
    )(idx, *normed, w_in)


def block_of(idx, k):
    return lax.rem(idx[0] - k + 4, 4) * 8 + idx[1] * 2 + idx[2]


WHOLE = [(j % 4, j // 4, 0, 4) for j in range(8)]
NEAR = [(0, 0, 0, 4), (1, 0, 0, 4), (3, 0, 0, 4), (0, 1, 0, 4), (1, 1, 0, 4), (3, 1, 0, 4)]


def assemble(idx, pieces, places, outs):
    for piece, (back, other, first, count) in zip(pieces, places, strict=True):
        at_y = lax.rem(idx[1] - back + 4, 4)
        at_core = 1 - idx[2] if other else idx[2]
        for i in range(count):
            block = lax.rem(idx[0] - first - i + 4, 4) * 8 + at_y * 2 + at_core
            where = pl.ds(pl.multiple_of(block * ROWS, ROWS), ROWS)
            for ref, column in outs:
                ref[where, :] = piece[i, :, column : column + DH]


def for_items(lows, highs, body):
    ends, total = [], jnp.int32(0)
    for low, high in zip(lows, highs, strict=True):
        total = total + (high - low + 1)
        ends.append(total)

    def step(i, carry):
        for j in range(PAIR):
            n = i * PAIR + j
            k, t = jnp.int32(0), n + lows[0]
            for q in range(1, 4):
                k = jnp.where(n >= ends[q - 1], q, k)
                t = jnp.where(n >= ends[q - 1], n - ends[q - 1] + lows[q], t)
            body(k, t, n < total)
        return carry

    lax.fori_loop(0, (total + PAIR - 1) // PAIR, step, 0)


def tile_at(t):
    return pl.ds(pl.multiple_of(jnp.minimum(t, TOKENS // TILE - 1) * TILE, TILE), TILE)


def set_marks(idx, hist, marks):
    row = lax.broadcasted_iota(jnp.int32, (ROWS, 128), 0)
    lows, highs = [], []
    for k in range(4):
        first = block_of(idx, k) * ROWS
        start, limit = hist.range_of(first + row)
        marks[0, k], marks[1, k] = start, limit
        lows.append(hist.pick(hist.starts, first) // TILE)
        highs.append(first // TILE)
    return lows, highs


def seen_by(idx, marks, k, t):
    row = lax.broadcasted_iota(jnp.int32, (ROWS, TILE), 0)
    lane = lax.broadcasted_iota(jnp.int32, (ROWS, TILE), 1)
    key = lane + t * TILE
    start, limit = [jnp.concatenate([marks[i, k]] * (TILE // 128), axis=1) for i in range(2)]
    return ((key >= start) & (key < limit)) | (key - row == block_of(idx, k) * ROWS)


def attend(idx, marks, q_own, total, k, t, keys, values):
    half = dot_t(q_own[k], keys) * (0.5 * DH**-0.5)
    weight = half * (1.0 + jnp.tanh(half))
    weight = jnp.where(seen_by(idx, marks, k, t), weight, 0.0).astype(bf16)
    total[k] += dot(weight, values)


def near_kernel(idx, len_ref, tgt_ref, *refs):
    pieces, out, all_hbm = refs[0:6], refs[6], refs[7:10]
    k_all, v_all, q_all, q_own, marks, sems = refs[10:16]
    hist = Histories(len_ref, tgt_ref)
    for x in range(4):
        at = pl.ds(pl.multiple_of((x * 4 + lax.rem(idx[1] + 2, 4)) * TILE, TILE), TILE)
        for ref in (k_all, v_all, q_all):
            ref[at, :] = jnp.zeros((TILE, DH), bf16)
    assemble(idx, pieces, NEAR, [(k_all, 0), (v_all, DH), (q_all, 2 * DH)])
    copies = copy_all(
        [
            pltpu.make_async_copy(ref, all_hbm[i], sems.at[i])
            for i, ref in enumerate((k_all, v_all, q_all))
        ]
    )
    for k in range(4):
        q_own[k] = pieces[0][k, :, 2 * DH : 3 * DH]
    out[...] = jnp.zeros_like(out)
    lows, highs = set_marks(idx, hist, marks)
    base = 3 - lax.rem(idx[1] + 2, 4)
    lows = [(low + base) // 4 * 3 + jnp.minimum((low + base) % 4, 3) for low in lows]
    highs = [(high + base) // 4 * 3 + jnp.minimum((high + base) % 4, 2) for high in highs]

    def body(k, u, valid):
        t = u + u // 3 - base
        at = tile_at(t)
        attend(idx, marks, q_own, out, k, t, k_all[at, :], v_all[at, :])

    for_items(lows, highs, body)
    for copy in copies:
        copy.wait()


def attend_near(idx, lengths, targets, pieces):
    return pl.pallas_call(
        near_kernel,
        in_specs=[SMEM] * 3 + [VMEM] * 6,
        out_specs=[VMEM] + [HBM] * 3,
        out_shape=[shape((4, ROWS, DH), f32)] + [shape((TOKENS, DH), bf16)] * 3,
        scratch_shapes=[pltpu.VMEM((TOKENS, DH), bf16)] * 3
        + [
            pltpu.VMEM((4, ROWS, DH), bf16),
            pltpu.VMEM((2, 4, ROWS, 128), jnp.int32),
            pltpu.SemaphoreType.DMA((3,)),
        ],
        compiler_params=PARAMS,
        cost_estimate=cost(0.5),
        name="attend_near",
    )(idx, lengths, targets, *pieces)


def far_kernel(idx, len_ref, tgt_ref, *refs):
    held, pieces, near, o_refs, all_hbm = refs[0], refs[1:5], refs[5], refs[9:13], refs[13:16]
    k_far, v_far, q_far, q_own, total, marks, sems = refs[16:23]
    hist = Histories(len_ref, tgt_ref)
    far = lax.rem(idx[1] + 2, 4)
    for j in range(4):
        other, first = j // 2, j % 2 * 2
        at_core = 1 - idx[2] if other else idx[2]
        for i in range(2):
            x = lax.rem(idx[0] - first - i + 4, 4)
            where = pl.ds(pl.multiple_of(x * TILE + at_core * ROWS, ROWS), ROWS)
            for n, ref in enumerate((k_far, v_far, q_far)):
                ref[where, :] = pieces[j][i, :, n * DH : (n + 1) * DH]
    copies = []
    for x in range(4):
        at = pl.ds(pl.multiple_of((x * 4 + far) * TILE, TILE), TILE)
        for n, ref in enumerate((k_far, v_far, q_far)):
            tile = ref.at[x * TILE : (x + 1) * TILE, :]
            copies.append(pltpu.make_async_copy(tile, all_hbm[n].at[at, :], sems.at[x * 3 + n]))
    copy_all(copies)
    for k in range(4):
        q_own[k] = held[k, :, 2 * DH : 3 * DH]
    total[...] = near[...]
    lows, highs = set_marks(idx, hist, marks)
    lows = [(low - far + 3) // 4 for low in lows]
    highs = [(high - far + 4) // 4 - 1 for high in highs]

    def body(k, u, valid):
        at = pl.ds(pl.multiple_of(jnp.minimum(u, 3) * TILE, TILE), TILE)
        attend(idx, marks, q_own, total, k, u * 4 + far, k_far[at, :], v_far[at, :])

    for_items(lows, highs, body)
    for k in range(4):
        o_refs[k][...] = total[k] * (1.0 / DIVISOR)
    for copy in copies:
        copy.wait()


def attend_far(idx, lengths, targets, held, pieces, near, everything):
    return pl.pallas_call(
        far_kernel,
        in_specs=[SMEM] * 3 + [VMEM] * 6 + [HBM] * 3,
        out_specs=[VMEM] * 4 + [HBM] * 3,
        out_shape=[shape((ROWS, DH), f32)] * 4 + [shape((TOKENS, DH), bf16)] * 3,
        input_output_aliases={9: 4, 10: 5, 11: 6},
        scratch_shapes=[pltpu.VMEM((4 * TILE, DH), bf16)] * 3
        + [
            pltpu.VMEM((4, ROWS, DH), bf16),
            pltpu.VMEM((4, ROWS, DH), f32),
            pltpu.VMEM((2, 4, ROWS, 128), jnp.int32),
            pltpu.SemaphoreType.DMA((12,)),
        ],
        compiler_params=PARAMS,
        cost_estimate=cost(0.5),
        name="attend_far",
    )(idx, lengths, targets, held, *pieces, near, *everything)


def two_of(head):
    high = head.astype(bf16).astype(f32)
    return high, (head - high).astype(bf16).astype(f32)


def head_rows(head):
    return jnp.concatenate(list(two_of(head)) + [jnp.zeros((14, 256), f32)], axis=0).astype(bf16)


def head_of(rows):
    rows = rows.astype(f32)
    return rows[0:1] + rows[1:2]


def even_sum(v):
    return (v[0] + v[2]) + (v[1] + v[3])


ACTS = 512 + 1024 + 1024 + 256


def middle_kernel(idx, len_ref, tgt_ref, a0, a1, a2, a3, gate_ref, slope_ref, x_ref, w_out, w_score, head, grad, score, *refs):
    d_refs, g_full, acts, mid_ref = refs[0:4], refs[4], refs[5], refs[6]
    att, work = refs[7:9]
    for k, ref in enumerate((a0, a1, a2, a3)):
        at = pl.ds(pl.multiple_of(lax.rem(idx[0] + k, 4) * DH, DH), DH)
        att[:, at] = ref[...]
    onorm, inverse = norm_rows(att[...])
    gate = gate_ref[...].astype(f32)
    gated = (onorm * gate).astype(bf16)
    acts[0:ROWS, 0:512] = gated
    out_b = (x_ref[...].astype(f32) + dot(gated, w_out[...])).astype(bf16)
    acts[0:ROWS, 1536:2560] = out_b
    mid = dot(out_b, w_score[...])
    hist = Histories(len_ref, tgt_ref)
    own = ((idx[0] * 4 + idx[1]) * 2 + idx[2]) * ROWS
    pos = own + lax.broadcasted_iota(jnp.int32, (ROWS, 1), 0)
    diagonal = lax.broadcasted_iota(jnp.int32, (ROWS, ROWS), 0) == lax.broadcasted_iota(
        jnp.int32, (ROWS, ROWS), 1
    )
    column = jnp.sum(jnp.where(diagonal, score[...], 0.0), axis=1, keepdims=True)
    weight = jnp.where(pos >= hist.pick(hist.firsts, pos), column, 0.0)
    sigma = sigmoid(mid)
    head_part = jnp.sum(weight * (mid * sigma), axis=0, keepdims=True)
    d_mid = (weight * head[...] * (sigma * (1.0 + mid * (1.0 - sigma)))).astype(bf16)
    acts[0:ROWS, 2560:2816] = d_mid
    mid_ref[...] = d_mid
    total_b = (grad[...].astype(f32) + dot_t(d_mid, w_score[...])).astype(bf16)
    acts[0:ROWS, 512:1536] = total_b
    d_gated = dot_t(total_b, w_out[...])
    att[...] = norm_back(d_gated * gate, onorm, inverse)
    work[...] = d_gated * onorm * slope_ref[...]
    g_full[...] = work[...].astype(bf16)
    for k in range(4):
        at = pl.ds(pl.multiple_of(lax.rem(idx[0] + k, 4) * DH, DH), DH)
        d_refs[k][0:ROWS, 0:DH] = att[:, at].astype(bf16)
        d_refs[k][0:ROWS, DH : 2 * DH] = work[:, at].astype(bf16)
        d_refs[k][ROWS : ROWS + 16, :] = head_rows(head_part)


def middle(idx, lengths, targets, attended, gate, slope, x, w_out, w_score, head, grad, score):
    width = HEADS * DH
    return pl.pallas_call(
        middle_kernel,
        in_specs=[SMEM] * 3 + [VMEM] * 12,
        out_specs=[VMEM] * 7,
        out_shape=[shape((ROWS + 16, 2 * DH), bf16)] * 4
        + [
            shape((ROWS, width), bf16),
            shape((ROWS, ACTS), bf16),
            shape((ROWS, 256), bf16),
        ],
        scratch_shapes=[pltpu.VMEM((ROWS, width), f32)] * 2,
        compiler_params=PARAMS,
        cost_estimate=cost(0.5),
        name="middle",
    )(idx, lengths, targets, *attended, gate, slope, x, w_out, w_score, head, grad, score)


SLOPE_SCALE = 0.5 * 2**-0.5
SLOPE_REST = DH**-0.5 / DIVISOR / 2**-0.5


def query_kernel(idx, len_ref, tgt_ref, *refs):
    held, d_refs, (k_all, v_all), out_refs = refs[0], refs[1:5], refs[5:7], refs[7:11]
    q_own, d_own, total, marks = refs[11:15]
    hist = Histories(len_ref, tgt_ref)
    for k in range(4):
        q_own[k] = held[k, :, 2 * DH : 3 * DH]
        d_own[k] = d_refs[k][0:ROWS, 0:DH]
    total[...] = jnp.zeros_like(total)
    lows, highs = set_marks(idx, hist, marks)

    def body(k, t, valid):
        at = tile_at(t)
        keys = k_all[at, :]
        half = dot_t(q_own[k], keys) * (0.5 * DH**-0.5)
        d_attn = dot_t(d_own[k], v_all[at, :])
        tanh = jnp.tanh(half)
        factor = (SLOPE_SCALE + SLOPE_SCALE * tanh) * (1.0 + half * (1.0 - tanh))
        d_raw = jnp.where(seen_by(idx, marks, k, t), d_attn * factor, 0.0).astype(bf16)
        total[k] += dot(d_raw, keys)

    for_items(lows, highs, body)
    for k in range(4):
        out_refs[k][...] = total[k] * SLOPE_REST


def query_grads(idx, lengths, targets, held, d_att, k_all, v_all):
    return pl.pallas_call(
        query_kernel,
        in_specs=[SMEM] * 3 + [VMEM] * 7,
        out_specs=[VMEM] * 4,
        out_shape=[shape((ROWS, DH), f32)] * 4,
        scratch_shapes=[pltpu.VMEM((4, ROWS, DH), bf16)] * 2
        + [pltpu.VMEM((4, ROWS, DH), f32), pltpu.VMEM((2, 4, ROWS, 128), jnp.int32)],
        compiler_params=PARAMS,
        cost_estimate=cost(3),
        name="query_grads",
    )(idx, lengths, targets, held, *d_att, k_all, v_all)


def key_kernel(idx, len_ref, tgt_ref, *refs):
    d_pieces, (k_hbm, v_hbm, q_hbm, slope_ref) = refs[0:8], refs[8:12]
    dq_refs, d_refs, back_refs, (all_ref, head_ref) = refs[12:16], refs[16:20], refs[20:24], refs[24:26]
    q_all, d_all, k_own, v_own, d_key, d_value, sems = refs[26:33]
    copies = [pltpu.make_async_copy(q_hbm, q_all, sems.at[8])]
    for k in range(4):
        at = pl.ds(pl.multiple_of(block_of(idx, k) * ROWS, ROWS), ROWS)
        copies.append(pltpu.make_async_copy(k_hbm.at[at, :], k_own.at[k], sems.at[k]))
        copies.append(pltpu.make_async_copy(v_hbm.at[at, :], v_own.at[k], sems.at[k + 4]))
    copy_all(copies)
    hist = Histories(len_ref, tgt_ref)
    heads = []
    for j, piece in enumerate(d_pieces):
        at_core = 1 - idx[2] if j >= 4 else idx[2]
        for k in range(4):
            block = lax.rem(idx[0] - k + 4, 4) * 8 + lax.rem(idx[1] - j % 4 + 4, 4) * 2 + at_core
            where = pl.ds(pl.multiple_of(block * ROWS, ROWS), ROWS)
            d_all[where, :] = piece[k * ROWS : (k + 1) * ROWS, :]
        rows = [piece[4 * ROWS + i * 16 : 4 * ROWS + (i + 1) * 16, :] for i in range(2)]
        heads.append(jnp.concatenate([head_of(row) for row in rows], axis=1))
    head_ref[...] = even_sum(heads[0:4]) + even_sum(heads[4:8])
    d_key[...] = jnp.zeros_like(d_key)
    d_value[...] = jnp.zeros_like(d_value)
    row = lax.broadcasted_iota(jnp.int32, (ROWS, TILE), 0)
    lane = lax.broadcasted_iota(jnp.int32, (1, TILE), 1)
    lows, highs = [], []
    for k in range(4):
        first = block_of(idx, k) * ROWS
        lows.append(first // TILE)
        highs.append((hist.pick(hist.ends, first + ROWS - 1) - 1) // TILE)
    for copy in copies:
        copy.wait()

    def body(k, t, valid):
        at = tile_at(t)
        queries, d_att = q_all[at, :], d_all[at, :]
        half = dot_t(k_own[k], queries) * (0.5 * DH**-0.5)
        d_attn = dot_t(v_own[k], d_att)
        key = block_of(idx, k) * ROWS + row
        pos = lane + t * TILE
        start, limit = hist.range_of(pos)
        start = start + jnp.where(valid, 0, TOKENS)
        seen = ((key >= start) & (key < limit)) | (key == pos)
        tanh = jnp.tanh(half)
        more = 1.0 + tanh
        weight = jnp.where(seen, half * more, 0.0).astype(bf16)
        factor = (SLOPE_SCALE * more) * (1.0 + half * (1.0 - tanh))
        d_raw = jnp.where(seen, d_attn * factor, 0.0).astype(bf16)
        d_key[k] += dot(d_raw, queries)
        d_value[k] += dot(weight, d_att)

    for_items(lows, highs, body)
    for k in range(4):
        d_q = (dq_refs[k][...] * slope_ref[k, :, 0:DH]).astype(bf16)
        d_k = (d_key[k] * SLOPE_REST * slope_ref[k, :, DH : 2 * DH]).astype(bf16)
        d_v = (d_value[k] * (1.0 / DIVISOR) * slope_ref[k, :, 2 * DH : 3 * DH]).astype(bf16)
        back_refs[k][:, 0:DH] = d_v
        back_refs[k][:, DH : 2 * DH] = d_q
        back_refs[k][:, 2 * DH : 3 * DH] = d_k
        at = pl.ds(k * ROWS, ROWS)
        all_ref[at, 0:DH] = d_refs[k][0:ROWS, DH : 2 * DH]
        all_ref[at, DH : 2 * DH] = d_v
        all_ref[at, 2 * DH : 3 * DH] = d_q
        all_ref[at, 3 * DH : 4 * DH] = d_k


def key_grads(idx, lengths, targets, d_pieces, everything, slope, d_query, d_att):
    return pl.pallas_call(
        key_kernel,
        in_specs=[SMEM] * 3 + [VMEM] * 8 + [HBM] * 3 + [VMEM] * 9,
        out_specs=[VMEM] * 6,
        out_shape=[shape((ROWS, 3 * DH), bf16)] * 4
        + [shape((4 * ROWS, 4 * DH), bf16), shape((1, 256), f32)],
        scratch_shapes=[pltpu.VMEM((TOKENS, DH), bf16)] * 2
        + [pltpu.VMEM((4, ROWS, DH), bf16)] * 2
        + [pltpu.VMEM((4, ROWS, DH), f32)] * 2
        + [pltpu.SemaphoreType.DMA((9,))],
        compiler_params=PARAMS,
        cost_estimate=cost(0.02),
        name="key_grads",
    )(idx, lengths, targets, *d_pieces, *everything, slope, *d_query, *d_att)


def dot_first(a, b):
    return lax.dot_general(a, b, (((0,), (0,)), ((), ())), preferred_element_type=f32)


def parts_kernel(idx, own, got, out, rows):
    rows[0:ROWS, :] = own[...]
    rows[ROWS : 2 * ROWS, :] = got[...]
    total = rows[:, pl.ds(pl.multiple_of(512 + idx[2] * 512, 512), 512)]
    d_mid = rows[:, pl.ds(pl.multiple_of(2560 + idx[2] * 128, 128), 128)]
    for x in range(4):
        part = dot_first(rows[:, x * 128 : (x + 1) * 128], total)
        score = dot_first(rows[:, 1536 + x * 256 : 1792 + x * 256], d_mid)
        for m in range(8):
            own_part = part[m * 16 : (m + 1) * 16]
            last = [score[m * 32 + j * 16 : m * 32 + (j + 1) * 16] for j in range(2)]
            block = [own_part[:, 0:256], own_part[:, 256:512], jnp.concatenate(last, axis=1)]
            out[x * 8 + m] = jnp.concatenate(block, axis=0).astype(bf16)


def parts(idx, own, got):
    return pl.pallas_call(
        parts_kernel,
        in_specs=[SMEM] + [VMEM] * 2,
        out_specs=VMEM,
        out_shape=shape((32, 48, 256), bf16),
        scratch_shapes=[pltpu.VMEM((2 * ROWS, ACTS), bf16)],
        compiler_params=PARAMS,
        cost_estimate=cost(0.3),
        name="parts",
    )(idx, own, got)


def weights_kernel(away, idx, n0, n1, n2, n3, d_pre, out, left):
    for k, ref in enumerate((n0, n1, n2, n3)):
        left[k * ROWS : (k + 1) * ROWS, :] = ref[...]
    half = idx[2] if away == 0 else 1 - idx[2]
    right = d_pre[:, pl.ds(pl.multiple_of(half * 256, 256), 256)]
    for n in range(4):
        part = dot_first(left[:, n * 256 : (n + 1) * 256], right)
        for i in range(8):
            out[n * 8 + i] = part[i * 32 : (i + 1) * 32].astype(out.dtype)


def weights(away, idx, normed, d_pre):
    return pl.pallas_call(
        functools.partial(weights_kernel, away),
        in_specs=[SMEM] + [VMEM] * 5,
        out_specs=VMEM,
        out_shape=shape((32, 32, 256), bf16 if away else f32),
        scratch_shapes=[pltpu.VMEM((512, 1024), bf16)],
        compiler_params=PARAMS,
        cost_estimate=cost(0.02),
        name="weights",
    )(idx, *normed, d_pre)


def merge_kernel(keep, got, early, out):
    for n in range(32):
        out[n, 0:32, :] = (keep[n] + got[n].astype(f32)).astype(bf16)
        out[n, 32:80, :] = early[n]


def merge(keep, got, early):
    return pl.pallas_call(
        merge_kernel,
        in_specs=[VMEM] * 3,
        out_specs=VMEM,
        out_shape=shape((32, 80, 256), bf16),
        compiler_params=PARAMS,
        cost_estimate=cost(0.3),
        name="merge",
    )(keep, got, early)


def pack_kernel(ref, head_ref, out_ref):
    for c in range(2):
        for h in range(HEADS):
            total = ref[h * 8 + c, 0:32, :].astype(f32)
            for n in range(1, 4):
                total = total + ref[h * 8 + n * 2 + c, 0:32, :].astype(f32)
            for i in range(2):
                z, half = divmod((c * 2 + i) * HEADS + h, 2)
                rows = total[:, i * 128 : (i + 1) * 128].astype(bf16)
                out_ref[z, half * 32 : (half + 1) * 32, :] = rows
    sums = []
    for c in range(2):
        total = ref[c, 32:80, :].astype(f32)
        for n in range(c + 2, 32, 2):
            total = total + ref[n, 32:80, :].astype(f32)
        sums.append(total)
    high, low = two_of(head_ref[...])
    head = [high[:, 0:128], high[:, 128:256], low[:, 0:128], low[:, 128:256]]
    head = jnp.concatenate(head + [jnp.zeros((4, 128), f32)], axis=0)
    for z in range(8):
        total, first, at = sums[z // 4], z % 4 // 2 * 16, z % 2 * 128
        score = [
            total[32 + i * 8 : 40 + i * 8, j * 128 + z % 4 * 32 : j * 128 + z % 4 * 32 + 32]
            for j in range(2)
            for i in range(2)
        ]
        rows = [total[first : first + 16, at : at + 128], jnp.concatenate(score, axis=1), head]
        out_ref[z, 64:96, :] = jnp.concatenate(rows, axis=0).astype(bf16)


def pack(value, head):
    return pl.pallas_call(
        pack_kernel,
        in_specs=[VMEM] * 2,
        out_specs=VMEM,
        out_shape=shape((8, 96, 128), bf16),
        compiler_params=PARAMS,
        cost_estimate=cost(2),
        name="pack",
    )(value, head)


def last_kernel(ref, in_ref, out_ref, score_ref, head_ref):
    total = ref[0].astype(f32)
    for z in range(1, 8):
        total = total + ref[z].astype(f32)
    in_ref[:, 0:128] = total[0:32]
    in_ref[:, 128:256] = total[32:64]
    out_ref[...] = total[64:80]
    for j in range(4):
        score_ref[j * 8 : (j + 1) * 8, :] = total[80:88, j * 32 : (j + 1) * 32]
    head_ref[:, 0:128] = total[88:89] + total[90:91]
    head_ref[:, 128:256] = total[89:90] + total[91:92]


def last_sum(value):
    return pl.pallas_call(
        last_kernel,
        in_specs=[VMEM],
        out_specs=[VMEM] * 4,
        out_shape=[
            shape((32, 256), f32),
            shape((16, 128), f32),
            shape((32, 32), f32),
            shape((1, 256), f32),
        ],
        compiler_params=PARAMS,
        cost_estimate=cost(1),
        name="last_sum",
    )(value)


def input_kernel(idx, b0, b1, b2, b3, gate_ref, w_ref, x_ref, grad, d_mid, w_score, out_ref, d_pre, d_norm):
    step = pl.program_id(0)
    width = HEADS * DH

    @pl.when(step == 0)
    def _():
        d_pre[:, 0:width] = gate_ref[...]
        for k, ref in enumerate((b0, b1, b2, b3)):
            head = lax.rem(idx[0] + k, 4)
            for kind in range(3):
                at = pl.ds(pl.multiple_of((kind + 1) * width + head * DH, DH), DH)
                d_pre[:, at] = ref[:, kind * DH : (kind + 1) * DH]

    d_norm[:, pl.ds(pl.multiple_of(step * 256, 256), 256)] = dot_t(d_pre[...], w_ref[...])

    @pl.when(step == 3)
    def _():
        normed, inverse = norm_rows(x_ref[...].astype(f32))
        d_total = grad[...].astype(f32) + dot_t(d_mid[...], w_score[...])
        out_ref[...] = (d_total + norm_back(d_norm[...], normed, inverse)).astype(bf16)


def input_grads(idx, back, gate, w_in, x, grad, d_mid, w_score):
    whole = lambda dims: pl.BlockSpec(dims, lambda i: (0, 0))
    return pl.pallas_call(
        input_kernel,
        grid=(4,),
        in_specs=[SMEM]
        + [whole((ROWS, 3 * DH))] * 4
        + [
            whole((ROWS, HEADS * DH)),
            pl.BlockSpec((256, 2048), lambda i: (i, 0)),
            whole((ROWS, 1024)),
            whole((ROWS, 1024)),
            whole((ROWS, 256)),
            whole((1024, 256)),
        ],
        out_specs=whole((ROWS, 1024)),
        out_shape=shape((ROWS, 1024), bf16),
        scratch_shapes=[pltpu.VMEM((ROWS, 2048), bf16), pltpu.VMEM((ROWS, 1024), f32)],
        compiler_params=PARAMS,
        cost_estimate=cost(4),
        name="input_grads",
    )(idx, *back, gate, w_in, x, grad, d_mid, w_score)


def join_kernel(*refs):
    for k in range(4):
        refs[4][k] = refs[k][:, 0 : refs[4].shape[2]]


def join(arrays, width):
    return pl.pallas_call(
        join_kernel,
        in_specs=[VMEM] * 4,
        out_specs=VMEM,
        out_shape=shape((4, ROWS, width), bf16),
        compiler_params=PARAMS,
        cost_estimate=cost(0.1),
        name="join",
    )(*arrays)


def own_kernel(d0, d1, d2, d3, out):
    refs = (d0, d1, d2, d3)
    for k in range(4):
        out[k * ROWS : (k + 1) * ROWS, :] = refs[k][0:ROWS, 0:DH]
    rows = head_rows(even_sum([head_of(ref[ROWS : ROWS + 16, :]) for ref in refs]))
    out[4 * ROWS : 4 * ROWS + 16, :] = rows[:, 0:DH]
    out[4 * ROWS + 16 : 4 * ROWS + 32, :] = rows[:, DH : 2 * DH]


def own_rows(d_att):
    return pl.pallas_call(
        own_kernel,
        in_specs=[VMEM] * 4,
        out_specs=VMEM,
        out_shape=shape((4 * ROWS + 32, DH), bf16),
        compiler_params=PARAMS,
        cost_estimate=cost(0.1),
        name="own_rows",
    )(*d_att)


def halves_kernel(back, ahead, low, high):
    low[...] = back[0:2]
    high[...] = ahead[2:4]


def halves(back, ahead):
    return pl.pallas_call(
        halves_kernel,
        in_specs=[VMEM] * 2,
        out_specs=[VMEM] * 2,
        out_shape=[shape((2,) + back.shape[1:], bf16)] * 2,
        compiler_params=PARAMS,
        cost_estimate=cost(0.1),
        name="halves",
    )(back, ahead)


def shifted(value, axis, by):
    size = lax.axis_size(axis)
    return lax.ppermute(value, axis, [(i, (i + by) % size) for i in range(size)])


def swapped(value, axis, bit):
    return lax.ppermute(value, axis, [(i, i ^ bit) for i in range(lax.axis_size(axis))])


def after(value, other):
    return lax.optimization_barrier((value, other))[0]


def exchange(values, sign):
    return [values[0]] + [shifted(values[k], "x", sign * k) for k in range(1, 4)]


def with_core(pieces):
    return pieces + [swapped(piece, "core", 1) for piece in pieces]


def gathered_ring(value):
    near = [value, shifted(value, "y", 1), shifted(value, "y", -1)]
    low, high = halves(near[1], near[2])
    far = [shifted(low, "y", 1), shifted(high, "y", -1)]
    return with_core(near), far


def on_device(x_rows, lengths, targets, w_in, w_out, w_score, head_score, grad_out, grad_score):
    x, lengths, targets = x_rows[0], lengths[0], targets[0]
    idx = jnp.stack([lax.axis_index(a) for a in SEQ]).astype(jnp.int32)
    normed, kvq = project(x, w_in)
    kvq = exchange(kvq, 1)
    held = join(kvq, 3 * DH)
    near_pieces, far_pieces = gathered_ring(held)
    normed = after(normed, kvq[3])
    near = [shifted(normed, "x", 1), shifted(normed, "x", -1)]
    normed_all = [normed, near[0], shifted(after(normed, near), "x", 2), near[1]]
    partly = attend_near(idx, lengths, targets, near_pieces)
    far_pieces, near, partly = lax.optimization_barrier((far_pieces, near, partly))
    far_pieces = with_core(far_pieces)
    forwarded = attend_far(idx, lengths, targets, held, far_pieces, partly[0], partly[1:4])
    k_all, v_all, q_all = forwarded[4:7]
    attended = exchange(forwarded[0:4], -1)
    gate, gate_slope = gates(after(normed, forwarded[0]), w_in)
    slope = slopes(idx, after(normed_all, forwarded[0]), w_in)
    attended = after(attended, slope)
    mid = middle(
        idx, lengths, targets, attended, gate, gate_slope, x, w_out, w_score,
        head_score.reshape(1, 256), grad_out[0], grad_score,
    )
    gate_full, acts, d_mid = mid[4:7]
    d_att = exchange(mid[0:4], 1)
    acts_other = swapped(after(acts, d_att), "core", 1)
    d_own = own_rows(d_att)
    late = [shifted(d_own, "y", k) for k in range(1, 4)]
    d_query = query_grads(idx, lengths, targets, held, d_att, k_all, v_all)
    d_pieces = with_core([d_own] + after(late, d_query[0]))
    keyed = key_grads(
        idx, lengths, targets, d_pieces, (k_all, v_all, q_all), slope, d_query, d_att
    )
    send = weights(1, idx, normed_all, keyed[4])
    got = swapped(send, "core", 1)
    keep = weights(0, idx, normed_all, after(keyed[4], send))
    early = parts(idx, after(acts, send), acts_other)
    partial = merge(keep, got, early)
    back, partial = lax.optimization_barrier((keyed[0:4], partial))
    partial = lax.all_to_all(partial, SEQ, 0, 0, tiled=True)
    back = exchange(back, -1)
    d_x = input_grads(idx, back, gate_full, w_in, x, grad_out[0], d_mid, w_score)
    last = lax.all_to_all(pack(partial, keyed[5]), "dp", 0, 0, tiled=True)
    d_w_in, d_w_out, d_w_score, d_head = last_sum(last)
    return d_x[None], d_w_in, d_w_out, d_w_score, d_head.reshape(256)


def solution(mesh):
    inner = Mesh(mesh.devices.reshape(8, 4, 4, 2), ("dp", "x", "y", "core"))
    placed = (
        P("dp", SEQ, None),
        P("dp", None),
        P("dp", None),
        P(),
        P(),
        P(),
        P(),
        P("dp", SEQ, None),
        P("dp", SEQ),
    )
    return jax.shard_map(
        on_device,
        mesh=inner,
        in_specs=placed,
        out_specs=(P("dp", SEQ, None), P(SEQ, "dp"), P(SEQ, "dp"), P(SEQ, "dp"), P()),
        check_vma=False,
    )
```
